32 devices in a mesh: flake: 2 (over y), trow: 16 (over z, x, core).
Axes of the slice: x: 2, y: 2, z: 4, core: 2. Of those that a mesh axis runs over, the one named last changes fastest.
Arguments:
- green: bfloat16 [192, 9, 4, 128, 128], P(('flake', 'trow')), parts along dimension 0, may hold values from -6 to 6
- integrals: bfloat16 [192, 9, 128, 128], P(('flake', 'trow')), parts along dimension 0, may hold values from -2 to 2
- pattern: int32 [192, 9], P(('flake', 'trow')), parts along dimension 0, may hold values from 0 to 1, as said below
- coefficients: bfloat16 [24576, 512], P(('flake', 'trow')), parts along dimension 0, may hold values from -0.0546875 to 0.0546875
Outputs:
- sigma_freq: float32 [2, 128, 1024, 512], P(None, None, ('flake', 'trow')), parts along dimension 2
The draws below stay inside these ranges and needn't reach their ends.
There are 2 independent parts, one for each index of `flake`. The reference program is written for one: setup_inputs(seed, part) draws one part's arguments, and reference() takes and returns one part's arrays. A program takes and returns all parts, laid end to end along the dimension named above; each array names one. Nothing has to cross between parts.
Inputs may be any that keep to these rules, and one draw needn't show every extreme that they name: pattern[r, s] is 1 where tile row r holds the tile of column r + s - 4; the diagonal slot s = 4 is always 1, and tile row 0 has all 9 slots.
All inputs are finite; a program needn't handle non-finite values.
Results may differ from the reference program's by a relative error of at most 0.005.
Values may be sent and summed in bfloat16 or wider, within the bound.
No kernel may reach another device: no remote copies, remote signals or barrier semaphores. Data moves between devices by JAX's collectives and lax.ppermute only.
A program may use at most 192 MiB of HBM per device.

```python
import jax
import jax.numpy as jnp
from jax import lax

TILE = 128
BAND = 4
TAU = 4
NMO = 512
NW = 128
TROW_DEV = 6
SLOTS = 9
NT = 96
NAO = 12288
N_TROW = 16


def draw_pattern(key, part):
    key = jax.random.fold_in(key, 7)
    full_key, count_key, order_key = jax.random.split(key, 3)
    dense_row = jax.random.randint(full_key, (NT,), 0, 20) < 3
    sparse_count = jax.random.randint(count_key, (NT,), 1, max(SLOTS // 3, 1) + 1)
    first_row = jnp.arange(NT, dtype=jnp.int32) == 0
    count = jnp.where(dense_row | first_row, SLOTS, sparse_count)
    row_keys = jax.random.split(order_key, NT)
    orders = jax.vmap(lambda single: jax.random.permutation(single, SLOTS))(row_keys)
    ranks = jnp.argsort(orders, axis=1, stable=True)
    slot_ids = jnp.arange(SLOTS, dtype=jnp.int32)[None, :]
    present = (ranks < count[:, None]) | (slot_ids == BAND)
    return present.astype(jnp.int32)


def steps_of(own_key, dims, shards, low, largest):
    factor_of, own = 1.0, jax.random.fold_in(own_key, 6)
    for dim, parts in shards:
        steps = jnp.exp(jax.random.uniform(jax.random.fold_in(own, dim), (parts,), jnp.float32, low / len(shards), largest / len(shards)))
        factor_of = factor_of * jnp.repeat(steps, dims[dim] // parts).reshape([-1 if axis == dim else 1 for axis in range(len(dims))])
    return factor_of


def gaussian(stream_key, extent, width, bound, pieces=(), kind=jnp.bfloat16):
    values = width * jax.random.normal(stream_key, extent, jnp.float32)
    if pieces:
        values = values * steps_of(stream_key, extent, pieces, -0.22, 0.18)
    return jnp.clip(values, -bound, bound).astype(kind)


def setup_inputs(seed: int = 0, part: int = 0) -> dict:
    keys = jax.random.split(jax.random.key(seed), 5)
    own_keys = jax.random.split(jax.random.fold_in(keys[4], part), 5)
    green = gaussian(own_keys[0], (NT, SLOTS, TAU, TILE, TILE), 1.0, 6.0, ((0, 16),))
    integrals = gaussian(own_keys[1], (NT, SLOTS, TILE, TILE), (TILE // 16) ** -0.5, 2.0, ((0, 16),))
    pattern = draw_pattern(jax.random.fold_in(jax.random.fold_in(keys[4], part), 71), part)
    coefficients = gaussian(own_keys[3], (NAO, NMO), NAO ** -0.5, 0.0546875, ((0, 16),))
    return dict(green=green, integrals=integrals, pattern=pattern, coefficients=coefficients)


def half_transform(green_rows, integral_rows, mask_rows, window):
    count = green_rows.shape[0]
    paired = (green_rows.astype(jnp.float32) * green_rows[:, :, ::-1].astype(jnp.float32)).astype(jnp.bfloat16)
    product = jnp.einsum("lstij,lsjk->lstik", paired.astype(jnp.float32), integral_rows.astype(jnp.float32))
    tiles = (product * mask_rows[:, :, None, None, None].astype(jnp.float32)).astype(jnp.bfloat16)
    total = jnp.zeros((count, TILE, TAU, NMO), jnp.float32)
    for slot in range(SLOTS):
        block = window[slot:slot + count]
        total = total + jnp.einsum("ltij,ljm->litm", tiles[:, slot].astype(jnp.float32), block.astype(jnp.float32))
    return total.reshape(count * TILE, TAU * NMO).astype(jnp.bfloat16)


def freq_tables():
    freq = jnp.arange(NW, dtype=jnp.float32)
    point = jnp.arange(TAU, dtype=jnp.float32)
    theta = jnp.pi * (2.0 * point + 1.0) / (2.0 * TAU)
    nodes = 0.5 * (1.0 - jnp.cos(theta))
    weights = (jnp.pi / (2.0 * TAU)) * jnp.sin(theta)
    angle = jnp.pi * (2.0 * freq[:, None] + 1.0) * nodes[None, :]
    return weights[None, :] * jnp.cos(angle), weights[None, :] * jnp.sin(angle)


def reference(green, integrals, pattern, coefficients):
    tiles = coefficients.reshape(NT, TILE, NMO)
    border = jnp.zeros((BAND, TILE, NMO), coefficients.dtype)
    padded = jnp.concatenate([border, tiles, border], axis=0)

    def block(total, index):
        start = (index * TROW_DEV).astype(jnp.int32)
        green_rows = lax.dynamic_slice_in_dim(green, start, TROW_DEV, 0)
        integral_rows = lax.dynamic_slice_in_dim(integrals, start, TROW_DEV, 0)
        mask_rows = lax.dynamic_slice_in_dim(pattern, start, TROW_DEV, 0)
        window = lax.dynamic_slice_in_dim(padded, start, TROW_DEV + 2 * BAND, 0)
        own = lax.dynamic_slice_in_dim(tiles, start, TROW_DEV, 0).reshape(TROW_DEV * TILE, NMO)
        half = half_transform(green_rows, integral_rows, mask_rows, window)
        term = lax.dot_general(own, half, (((0,), (0,)), ((), ())), preferred_element_type=jnp.float32)
        return total + term, None

    start_total = jnp.zeros((NMO, TAU * NMO), jnp.float32)
    total, _ = lax.scan(block, start_total, jnp.arange(N_TROW, dtype=jnp.int32))
    sigma_tau = total.reshape(NMO, TAU, NMO)
    cosine, sine = freq_tables()
    real_part = jnp.einsum("nk,akb->nab", cosine, sigma_tau, precision=lax.Precision.HIGHEST)
    imag_part = jnp.einsum("nk,akb->nab", sine, sigma_tau, precision=lax.Precision.HIGHEST)
    return jnp.stack([real_part, imag_part], axis=0)
```

```python
import functools

import jax
import jax.numpy as jnp
import numpy as np
from jax import lax
from jax.experimental import pallas as pl
from jax.experimental.pallas import tpu as pltpu
from jax.sharding import PartitionSpec as P

TILE = 128
BAND = 4
TAU = 4
PAIRS = TAU // 2
NMO = 512
NW = 128
SLOTS = 9
FREQ_BLOCK = 32
MIB = 1 << 20


def tiles_kernel(
    count, pattern, green, integrals, coefficients, near, part, far, transposed, gbuf, ibuf, window, sems, csems
):
    core = lax.rem(lax.axis_index("trow"), 2)
    first = core == 0
    low = jnp.where(first, BAND, 0)
    inside = count + BAND
    own_at = pl.multiple_of(jnp.where(first, 0, BAND * TILE), TILE)
    near_at = pl.multiple_of(jnp.where(first, count * TILE, 0), TILE)

    def green_copy(index):
        row, slot = index // SLOTS, index % SLOTS
        return (
            pltpu.make_async_copy(green.at[row, slot], gbuf.at[index], sems.at[index, 0]),
            pltpu.make_async_copy(integrals.at[row, slot], ibuf.at[index], sems.at[index, 1]),
        )

    own_copy = pltpu.make_async_copy(coefficients, window.at[pl.ds(own_at, count * TILE)], csems.at[0])
    near_copy = pltpu.make_async_copy(near, window.at[pl.ds(near_at, BAND * TILE)], csems.at[1])
    own_copy.start()
    near_copy.start()

    @pl.loop(0, count * SLOTS)
    def _(index):
        @pl.when(pattern[index // SLOTS, index % SLOTS] != 0)
        def _():
            for copy in green_copy(index):
                copy.start()

    part[...] = jnp.zeros_like(part)
    far[...] = jnp.zeros_like(far)
    own_copy.wait()
    near_copy.wait()
    for row in range(count):
        block = window[pl.ds(pl.multiple_of(own_at + row * TILE, TILE), TILE), :]
        transposed[:, row * TILE : (row + 1) * TILE] = block.T

    @pl.loop(0, count * SLOTS)
    def _(index):
        row, slot = index // SLOTS, index % SLOTS

        @pl.when(pattern[row, slot] != 0)
        def _():
            for copy in green_copy(index):
                copy.wait()
            pairs = [
                (gbuf[index, t].astype(jnp.float32) * gbuf[index, TAU - 1 - t].astype(jnp.float32)).astype(jnp.bfloat16)
                for t in range(PAIRS)
            ]
            sigma = jnp.dot(
                jnp.concatenate(pairs, axis=0), ibuf[index], preferred_element_type=jnp.float32
            ).astype(jnp.bfloat16)
            place = row + slot - low
            here = (place >= 0) & (place < inside)

            @pl.when(here)
            def _():
                block = window[pl.ds(pl.multiple_of(place * TILE, TILE), TILE), :]
                part[row] += jnp.dot(sigma, block, preferred_element_type=jnp.float32)

            @pl.when(jnp.logical_not(here))
            def _():
                queue = jnp.where(first, row, row - (count - BAND))
                tile = jnp.where(first, row + slot, row + slot - inside)
                far[queue, tile] = sigma


def tiles(green, integrals, pattern, coefficients, near):
    count = green.shape[0]
    anywhere = pl.BlockSpec(memory_space=pl.ANY)
    vmem = pl.BlockSpec(memory_space=pltpu.VMEM)
    return pl.pallas_call(
        functools.partial(tiles_kernel, count),
        out_shape=(
            pltpu.VMEM((count, PAIRS * TILE, NMO), jnp.float32),
            pltpu.VMEM((BAND, BAND, PAIRS * TILE, TILE), jnp.bfloat16),
            pltpu.VMEM((NMO, count * TILE), jnp.bfloat16),
        ),
        in_specs=[pl.BlockSpec(memory_space=pltpu.SMEM)] + [anywhere] * 4,
        out_specs=(vmem, vmem, vmem),
        scratch_shapes=[
            pltpu.VMEM((count * SLOTS, TAU, TILE, TILE), jnp.bfloat16),
            pltpu.VMEM((count * SLOTS, TILE, TILE), jnp.bfloat16),
            pltpu.VMEM(((count + BAND) * TILE, NMO), jnp.bfloat16),
            pltpu.SemaphoreType.DMA((count * SLOTS, 2)),
            pltpu.SemaphoreType.DMA((2,)),
        ],
        compiler_params=pltpu.CompilerParams(vmem_limit_bytes=24 * MIB),
        cost_estimate=pl.CostEstimate(flops=2_000_000_000, bytes_accessed=12_000_000, transcendentals=0),
        name="tiles",
    )(pattern, green, integrals, coefficients, near)


def project_kernel(count, split, part, far, halo, transposed, *refs):
    outs, half = refs[:-1], refs[-1]
    me = lax.axis_index("trow")
    first = lax.rem(me, 2) == 0
    start = jnp.where(first, 0, count - BAND)

    def store(row, value):
        rows = pl.ds(pl.multiple_of(row * TILE, TILE), TILE)
        for t in range(PAIRS):
            half[t, rows, :] = value[t * TILE : (t + 1) * TILE].astype(jnp.bfloat16)

    for queue in range(BAND):
        sigma = jnp.concatenate([far[queue, tile] for tile in range(BAND)], axis=1)
        store(start + queue, part[start + queue] + jnp.dot(sigma, halo[...], preferred_element_type=jnp.float32))
    for rest in range(count - BAND):
        row = jnp.where(first, BAND + rest, rest)
        store(row, part[row])
    chunks = NMO // TILE
    for k in range(chunks):
        chunk = lax.bitwise_xor(lax.div(me, 4), k) if split else k
        lhs = transposed[pl.ds(pl.multiple_of(chunk * TILE, TILE), TILE), :]
        for t in range(PAIRS):
            columns = slice(t * NMO, (t + 1) * NMO)
            total = jnp.dot(lhs, half[t], preferred_element_type=jnp.float32)
            if split:
                keep, send = outs
                upper, lower = total[: TILE // 2], total[TILE // 2 :]
                keep[k, :, columns] = jnp.where(first, upper, lower)
                send[k, :, columns] = jnp.where(first, lower, upper).astype(jnp.bfloat16)
            else:
                outs[0][k * TILE : (k + 1) * TILE, columns] = total


def project(part, far, halo, transposed, split):
    count = part.shape[0]
    vmem = pl.BlockSpec(memory_space=pltpu.VMEM)
    if split:
        shape = (NMO // TILE, TILE // 2, PAIRS * NMO)
        out_shape = (pltpu.VMEM(shape, jnp.float32), pltpu.VMEM(shape, jnp.bfloat16))
    else:
        out_shape = (jax.ShapeDtypeStruct((NMO, PAIRS * NMO), jnp.float32),)
    return pl.pallas_call(
        functools.partial(project_kernel, count, split),
        out_shape=out_shape,
        in_specs=[vmem] * 4,
        out_specs=tuple(vmem for _ in out_shape),
        scratch_shapes=[pltpu.VMEM((PAIRS, count * TILE, NMO), jnp.bfloat16)],
        compiler_params=pltpu.CompilerParams(vmem_limit_bytes=24 * MIB),
        cost_estimate=pl.CostEstimate(flops=1_600_000_000, bytes_accessed=6_000_000, transcendentals=0),
        name="project",
    )(part, far, halo, transposed)


def freq_tables():
    point = np.arange(TAU, dtype=np.float32)
    freq = np.arange(NW, dtype=np.float32)
    pi = np.float32(np.pi)
    theta = pi * (np.float32(2.0) * point + np.float32(1.0)) / np.float32(2.0 * TAU)
    nodes = np.float32(0.5) * (np.float32(1.0) - np.cos(theta))
    weights = np.float32(np.pi / (2.0 * TAU)) * np.sin(theta)
    angle = pi * (np.float32(2.0) * freq[:, None] + np.float32(1.0)) * nodes[None, :]
    both = np.concatenate([weights[None, :] * np.cos(angle), weights[None, :] * np.sin(angle)], axis=0)
    folded = both[:, :PAIRS] + both[:, : PAIRS - 1 : -1]
    return folded.astype(np.float32).reshape(-1)


def frequency_kernel(table, mine, other, out):
    step = pl.program_id(0)
    points = [
        mine[:, t * NMO : (t + 1) * NMO] + other[:, t * NMO : (t + 1) * NMO] for t in range(PAIRS)
    ]

    @pl.loop(0, FREQ_BLOCK, unroll=4)
    def _(n):
        at = (step * FREQ_BLOCK + n) * PAIRS
        value = table[at] * points[0]
        for t in range(1, PAIRS):
            value = value + table[at + t] * points[t]
        out[n] = value


def frequency(mine, other):
    rows = mine.shape[0]
    whole = pl.BlockSpec((rows, PAIRS * NMO), lambda i: (0, 0))
    out = pl.pallas_call(
        frequency_kernel,
        grid=(2 * NW // FREQ_BLOCK,),
        out_shape=jax.ShapeDtypeStruct((2 * NW, rows, NMO), jnp.float32),
        in_specs=[pl.BlockSpec(memory_space=pltpu.SMEM), whole, whole],
        out_specs=pl.BlockSpec((FREQ_BLOCK, rows, NMO), lambda i: (i, 0, 0)),
        compiler_params=pltpu.CompilerParams(vmem_limit_bytes=24 * MIB),
        cost_estimate=pl.CostEstimate(flops=50_000_000, bytes_accessed=17_000_000, transcendentals=0),
        name="frequency",
    )(jnp.asarray(freq_tables()), mine, other)
    return out.reshape(2, NW, rows, NMO)


def local(devices, green, integrals, pattern, coefficients):
    rows = coefficients.shape[0]
    width = BAND * TILE
    core = lax.rem(lax.axis_index("trow"), 2)
    away = lax.dynamic_slice_in_dim(coefficients, core * (rows - width), width, axis=0)
    pairs = [(i, i + 1) for i in range(1, devices - 1, 2)]
    halo = lax.ppermute(away, "trow", pairs + [(b, a) for a, b in pairs])
    inner = lax.dynamic_slice_in_dim(coefficients, (1 - core) * (rows - width), width, axis=0)
    near = lax.ppermute(inner, "trow", [(i, i ^ 1) for i in range(devices)])
    part, far, transposed = tiles(green, integrals, pattern, coefficients, near)
    if devices != 16:
        (summed,) = project(part, far, halo, transposed, False)
        total = lax.psum_scatter(summed, "trow", scatter_dimension=0, tiled=True)
        return frequency(total, jnp.zeros_like(total))
    keep, send = project(part, far, halo, transposed, True)
    arrived = lax.ppermute(send, "trow", [(i, i ^ 1) for i in range(devices)])
    pieces = [(keep[k] + arrived[k].astype(jnp.float32)).astype(jnp.bfloat16) for k in range(4)]
    got = []
    for k in range(4):
        moves = []
        for i in range(devices):
            z, x, c = i // 4, i // 2 % 2, i % 2
            moves.append((i, ((z ^ k) * 2 + c) * 2 + x))
        got.append(lax.ppermute(pieces[k], "trow", moves))
    total = got[0].astype(jnp.float32)
    for piece in got[1:]:
        total = total + piece.astype(jnp.float32)
    count = total.shape[0] // 2
    mine = lax.dynamic_slice_in_dim(total, core * count, count, axis=0)
    other = lax.dynamic_slice_in_dim(total, (1 - core) * count, count, axis=0)
    other = lax.ppermute(other, "trow", [(i, i ^ 1) for i in range(devices)])
    return frequency(mine, other)


def solution(mesh):
    in_specs = (
        P(("flake", "trow"), None, None, None, None),
        P(("flake", "trow"), None, None, None),
        P(("flake", "trow"), None),
        P(("flake", "trow"), None),
    )
    out_specs = P(None, None, ("flake", "trow"), None)
    return jax.shard_map(
        functools.partial(local, mesh.shape["trow"]),
        mesh=mesh,
        in_specs=in_specs,
        out_specs=out_specs,
        check_vma=False,
    )
```

```python
import functools

import jax
import jax.numpy as jnp
import numpy as np
from jax import lax
from jax.experimental import pallas as pl
from jax.experimental.pallas import tpu as pltpu
from jax.sharding import PartitionSpec as P

TILE = 128
BAND = 4
TAU = 4
PAIRS = TAU // 2
NMO = 512
NW = 128
SLOTS = 9
FREQ_BLOCK = 16
GROUP = 4
MIB = 1 << 20


def tiles_kernel(
    count, pattern, green, integrals, coefficients, near, part, sigma, transposed, gbuf, ibuf, window, order, sems, csems
):
    first = lax.rem(lax.axis_index("trow"), 2) == 0
    inside = count + BAND
    own_at = pl.multiple_of(jnp.where(first, 0, BAND * TILE), TILE)
    near_at = pl.multiple_of(jnp.where(first, count * TILE, 0), TILE)

    def fetch(index):
        row, slot = index // SLOTS, index % SLOTS
        return (
            pltpu.make_async_copy(green.at[row, slot], gbuf.at[index], sems.at[index, 0]),
            pltpu.make_async_copy(integrals.at[row, slot], ibuf.at[index], sems.at[index, 1]),
        )

    def enlist(index, found):
        present = pattern[index // SLOTS, index % SLOTS] != 0

        @pl.when(present)
        def _():
            order[found] = index
            for copy in fetch(index):
                copy.start()

        return found + present.astype(jnp.int32)

    own_copy = pltpu.make_async_copy(coefficients, window.at[pl.ds(own_at, count * TILE)], csems.at[0])
    near_copy = pltpu.make_async_copy(near, window.at[pl.ds(near_at, BAND * TILE)], csems.at[1])
    own_copy.start()
    near_copy.start()
    found = lax.fori_loop(0, count * SLOTS, enlist, jnp.int32(0))
    for extra in range(GROUP - 1):
        order[found + extra] = order[found - 1]
    sigma[...] = jnp.zeros_like(sigma)
    own_copy.wait()
    for row in range(count):
        block = window[pl.ds(pl.multiple_of(own_at + row * TILE, TILE), TILE), :]
        transposed[:, row * TILE : (row + 1) * TILE] = block.T

    @pl.loop(0, pl.cdiv(found, GROUP))
    def _(group):
        indices = [order[group * GROUP + member] for member in range(GROUP)]
        for member, index in enumerate(indices):

            @pl.when(group * GROUP + member < found)
            def _():
                for copy in fetch(index):
                    copy.wait()

        for index in indices:
            paired = jnp.concatenate([gbuf[index, t] * gbuf[index, TAU - 1 - t] for t in range(PAIRS)], axis=0)
            product = jnp.dot(paired, ibuf[index], preferred_element_type=jnp.float32)
            sigma[index // SLOTS, index % SLOTS] = product.astype(jnp.bfloat16)

    near_copy.wait()

    def reduce_rows(low):
        for row in range(count):
            begin, end = max(0, low - row), min(SLOTS, low + inside - row)
            lhs = jnp.concatenate([sigma[row, slot] for slot in range(begin, end)], axis=1)
            rhs = window[(row + begin - low) * TILE : (row + end - low) * TILE, :]
            part[row] = jnp.dot(lhs, rhs, preferred_element_type=jnp.float32)

    @pl.when(first)
    def _():
        reduce_rows(BAND)

    @pl.when(jnp.logical_not(first))
    def _():
        reduce_rows(0)


def tiles(green, integrals, pattern, coefficients, near):
    count = green.shape[0]
    hbm = pl.BlockSpec(memory_space=pltpu.HBM)
    vmem = pl.BlockSpec(memory_space=pltpu.VMEM)
    placed = [pltpu.with_memory_space_constraint(x, pltpu.HBM) for x in (green, integrals, coefficients)]
    return pl.pallas_call(
        functools.partial(tiles_kernel, count),
        out_shape=(
            pltpu.VMEM((count, PAIRS * TILE, NMO), jnp.float32),
            pltpu.VMEM((count, SLOTS, PAIRS * TILE, TILE), jnp.bfloat16),
            pltpu.VMEM((NMO, count * TILE), jnp.bfloat16),
        ),
        in_specs=[pl.BlockSpec(memory_space=pltpu.SMEM), hbm, hbm, hbm, vmem],
        out_specs=(vmem, vmem, vmem),
        scratch_shapes=[
            pltpu.VMEM((count * SLOTS, TAU, TILE, TILE), jnp.bfloat16),
            pltpu.VMEM((count * SLOTS, TILE, TILE), jnp.bfloat16),
            pltpu.VMEM(((count + BAND) * TILE, NMO), jnp.bfloat16),
            pltpu.SMEM((count * SLOTS + GROUP,), jnp.int32),
            pltpu.SemaphoreType.DMA((count * SLOTS, 2)),
            pltpu.SemaphoreType.DMA((2,)),
        ],
        compiler_params=pltpu.CompilerParams(vmem_limit_bytes=24 * MIB),
        cost_estimate=pl.CostEstimate(flops=2_000_000_000, bytes_accessed=12_000_000, transcendentals=0),
        name="tiles",
    )(pattern, *placed, pltpu.with_memory_space_constraint(near, pltpu.VMEM))


def project_kernel(count, split, part, sigma, halo, transposed, *refs):
    outs, half = refs[:-1], refs[-1]
    me = lax.axis_index("trow")
    first = lax.rem(me, 2) == 0

    def store(row, value):
        for t in range(PAIRS):
            half[t, row * TILE : (row + 1) * TILE, :] = value[t * TILE : (t + 1) * TILE].astype(jnp.bfloat16)

    def add_far(low):
        for row in range(count):
            if low:
                slots = range(0, max(0, BAND - row))
                at = row
            else:
                slots = range(min(SLOTS, count + BAND - row), SLOTS)
                at = 0
            value = part[row]
            if slots:
                lhs = jnp.concatenate([sigma[row, slot] for slot in slots], axis=1)
                rhs = halo[at * TILE : (at + len(slots)) * TILE, :]
                value = value + jnp.dot(lhs, rhs, preferred_element_type=jnp.float32)
            store(row, value)

    @pl.when(first)
    def _():
        add_far(BAND)

    @pl.when(jnp.logical_not(first))
    def _():
        add_far(0)

    for k in range(NMO // TILE):
        chunk = lax.bitwise_xor(lax.div(me, 4), k) if split else k
        lhs = transposed[pl.ds(pl.multiple_of(chunk * TILE, TILE), TILE), :]
        for t in range(PAIRS):
            columns = slice(t * NMO, (t + 1) * NMO)
            total = jnp.dot(lhs, half[t], preferred_element_type=jnp.float32)
            if split:
                keep, send = outs
                upper, lower = total[: TILE // 2], total[TILE // 2 :]
                keep[k, :, columns] = jnp.where(first, upper, lower)
                send[k, :, columns] = jnp.where(first, lower, upper).astype(jnp.bfloat16)
            else:
                outs[0][k * TILE : (k + 1) * TILE, columns] = total


def project(part, sigma, halo, transposed, split):
    count = part.shape[0]
    vmem = pl.BlockSpec(memory_space=pltpu.VMEM)
    if split:
        shape = (NMO // TILE, TILE // 2, PAIRS * NMO)
        out_shape = (pltpu.VMEM(shape, jnp.float32), pltpu.VMEM(shape, jnp.bfloat16))
    else:
        out_shape = (jax.ShapeDtypeStruct((NMO, PAIRS * NMO), jnp.float32),)
    return pl.pallas_call(
        functools.partial(project_kernel, count, split),
        out_shape=out_shape,
        in_specs=[vmem] * 4,
        out_specs=tuple(vmem for _ in out_shape),
        scratch_shapes=[pltpu.VMEM((PAIRS, count * TILE, NMO), jnp.bfloat16)],
        compiler_params=pltpu.CompilerParams(vmem_limit_bytes=24 * MIB),
        cost_estimate=pl.CostEstimate(flops=1_600_000_000, bytes_accessed=6_000_000, transcendentals=0),
        name="project",
    )(*[pltpu.with_memory_space_constraint(x, pltpu.VMEM) for x in (part, sigma, halo, transposed)])


def freq_tables():
    point = np.arange(TAU, dtype=np.float32)
    freq = np.arange(NW, dtype=np.float32)
    pi = np.float32(np.pi)
    theta = pi * (np.float32(2.0) * point + np.float32(1.0)) / np.float32(2.0 * TAU)
    nodes = np.float32(0.5) * (np.float32(1.0) - np.cos(theta))
    weights = np.float32(np.pi / (2.0 * TAU)) * np.sin(theta)
    angle = pi * (np.float32(2.0) * freq[:, None] + np.float32(1.0)) * nodes[None, :]
    both = np.concatenate([weights[None, :] * np.cos(angle), weights[None, :] * np.sin(angle)], axis=0)
    folded = both[:, :PAIRS] + both[:, : PAIRS - 1 : -1]
    return folded.astype(np.float32).reshape(-1)


def frequency_kernel(table, mine, other, out, buffer, sems):
    points = [
        mine[:, t * NMO : (t + 1) * NMO] + other[:, t * NMO : (t + 1) * NMO] for t in range(PAIRS)
    ]

    def copy(step):
        rows = pl.ds(step * FREQ_BLOCK, FREQ_BLOCK)
        return pltpu.make_async_copy(buffer.at[rows], out.at[rows], sems.at[step])

    @pl.loop(0, 2 * NW // FREQ_BLOCK)
    def _(step):
        @pl.loop(0, FREQ_BLOCK, unroll=4)
        def _(n):
            at = (step * FREQ_BLOCK + n) * PAIRS
            value = table[at] * points[0]
            for t in range(1, PAIRS):
                value = value + table[at + t] * points[t]
            buffer[step * FREQ_BLOCK + n] = value

        copy(step).start()

    @pl.loop(0, 2 * NW // FREQ_BLOCK)
    def _(step):
        copy(step).wait()


def frequency(mine, other):
    rows = mine.shape[0]
    vmem = pl.BlockSpec(memory_space=pltpu.VMEM)
    out = pl.pallas_call(
        frequency_kernel,
        out_shape=jax.ShapeDtypeStruct((2 * NW, rows, NMO), jnp.float32),
        in_specs=[pl.BlockSpec(memory_space=pltpu.SMEM), vmem, vmem],
        out_specs=pl.BlockSpec(memory_space=pl.ANY),
        scratch_shapes=[
            pltpu.VMEM((2 * NW, rows, NMO), jnp.float32),
            pltpu.SemaphoreType.DMA((2 * NW // FREQ_BLOCK,)),
        ],
        compiler_params=pltpu.CompilerParams(vmem_limit_bytes=24 * MIB),
        cost_estimate=pl.CostEstimate(flops=50_000_000, bytes_accessed=17_000_000, transcendentals=0),
        name="frequency",
    )(jnp.asarray(freq_tables()), mine, other)
    return out.reshape(2, NW, rows, NMO)


def local(devices, green, integrals, pattern, coefficients):
    rows = coefficients.shape[0]
    width = BAND * TILE
    core = lax.rem(lax.axis_index("trow"), 2)
    away = lax.dynamic_slice_in_dim(coefficients, core * (rows - width), width, axis=0)
    pairs = [(i, i + 1) for i in range(1, devices - 1, 2)]
    halo = lax.ppermute(away, "trow", pairs + [(b, a) for a, b in pairs])
    inner = lax.dynamic_slice_in_dim(coefficients, (1 - core) * (rows - width), width, axis=0)
    near = lax.ppermute(inner, "trow", [(i, i ^ 1) for i in range(devices)])
    part, far, transposed = tiles(green, integrals, pattern, coefficients, near)
    if devices != 16:
        (summed,) = project(part, far, halo, transposed, False)
        total = lax.psum_scatter(summed, "trow", scatter_dimension=0, tiled=True)
        return frequency(total, jnp.zeros_like(total))
    keep, send = project(part, far, halo, transposed, True)
    arrived = lax.ppermute(send, "trow", [(i, i ^ 1) for i in range(devices)])
    pieces = [(keep[k] + arrived[k].astype(jnp.float32)).astype(jnp.bfloat16) for k in range(4)]
    got = []
    for k in range(4):
        moves = []
        for i in range(devices):
            z, x, c = i // 4, i // 2 % 2, i % 2
            moves.append((i, ((z ^ k) * 2 + c) * 2 + x))
        got.append(lax.ppermute(pieces[k], "trow", moves))
    total = got[0].astype(jnp.float32)
    for piece in got[1:]:
        total = total + piece.astype(jnp.float32)
    count = total.shape[0] // 2
    mine = lax.dynamic_slice_in_dim(total, core * count, count, axis=0)
    other = lax.dynamic_slice_in_dim(total, (1 - core) * count, count, axis=0)
    other = lax.ppermute(other, "trow", [(i, i ^ 1) for i in range(devices)])
    return frequency(mine, other)


def solution(mesh):
    in_specs = (
        P(("flake", "trow"), None, None, None, None),
        P(("flake", "trow"), None, None, None),
        P(("flake", "trow"), None),
        P(("flake", "trow"), None),
    )
    out_specs = P(None, None, ("flake", "trow"), None)
    return jax.shard_map(
        functools.partial(local, mesh.shape["trow"]),
        mesh=mesh,
        in_specs=in_specs,
        out_specs=out_specs,
        check_vma=False,
    )
```

```python
import functools

import jax
import jax.numpy as jnp
import numpy as np
from jax import lax
from jax.experimental import pallas as pl
from jax.experimental.pallas import tpu as pltpu
from jax.sharding import PartitionSpec as P

TILE = 128
BAND = 4
TAU = 4
PAIRS = TAU // 2
NMO = 512
NW = 128
SLOTS = 9
FREQ_BLOCK = 16
GROUP = 4
CHUNKS = 2
COLUMNS = NMO // CHUNKS
MIB = 1 << 20


def sides(count, row):
    return range(0, max(0, BAND - row)), range(max(0, BAND - row), min(SLOTS, count + BAND - row)), range(
        min(SLOTS, count + BAND - row), SLOTS
    )


def contract(sigma, row, slots, block, begin):
    lhs = jnp.concatenate([sigma[row, slot] for slot in slots], axis=1)
    rhs = block[begin * TILE : (begin + len(slots)) * TILE, :]
    return jnp.dot(lhs, rhs, preferred_element_type=jnp.float32)


def tiles_kernel(
    count,
    mask,
    green,
    integrals,
    coefficients,
    part,
    sigma,
    transposed,
    gbuf,
    ibuf,
    own,
    pattern,
    order,
    sems,
    csem,
):
    def fetch(index):
        row, slot = index // SLOTS, index % SLOTS
        return (
            pltpu.make_async_copy(green.at[row, slot], gbuf.at[index], sems.at[index, 0]),
            pltpu.make_async_copy(integrals.at[row, slot], ibuf.at[index], sems.at[index, 1]),
        )

    def enlist(index, found):
        present = pattern[index // SLOTS, index % SLOTS] != 0

        @pl.when(present)
        def _():
            order[found] = index
            for copy in fetch(index):
                copy.start()

        return found + present.astype(jnp.int32)

    mask_copy = pltpu.make_async_copy(mask, pattern, csem.at[0])
    own_copy = pltpu.make_async_copy(coefficients, own, csem.at[1])
    mask_copy.start()
    own_copy.start()
    sigma[...] = jnp.zeros_like(sigma)
    mask_copy.wait()
    found = lax.fori_loop(0, count * SLOTS, enlist, jnp.int32(0))
    for extra in range(GROUP - 1):
        order[found + extra] = order[found - 1]
    own_copy.wait()
    for row in range(count):
        rows = slice(row * TILE, (row + 1) * TILE)
        transposed[:, rows] = own[rows, :].T

    @pl.loop(0, pl.cdiv(found, GROUP))
    def _(group):
        indices = [order[group * GROUP + member] for member in range(GROUP)]
        for member, index in enumerate(indices):

            @pl.when(group * GROUP + member < found)
            def _():
                for copy in fetch(index):
                    copy.wait()

        for index in indices:
            paired = jnp.concatenate([gbuf[index, t] * gbuf[index, TAU - 1 - t] for t in range(PAIRS)], axis=0)
            product = jnp.dot(paired, ibuf[index], preferred_element_type=jnp.float32)
            sigma[index // SLOTS, index % SLOTS] = product.astype(jnp.bfloat16)

    for row in range(count):
        _, slots, _ = sides(count, row)
        part[row] = contract(sigma, row, slots, own, row + slots[0] - BAND)


def tiles(green, integrals, pattern, coefficients):
    count = green.shape[0]
    hbm = pl.BlockSpec(memory_space=pltpu.HBM)
    vmem = pl.BlockSpec(memory_space=pltpu.VMEM)
    placed = [pltpu.with_memory_space_constraint(x, pltpu.HBM) for x in (pattern, green, integrals, coefficients)]
    return pl.pallas_call(
        functools.partial(tiles_kernel, count),
        out_shape=(
            pltpu.VMEM((count, PAIRS * TILE, NMO), jnp.float32),
            pltpu.VMEM((count, SLOTS, PAIRS * TILE, TILE), jnp.bfloat16),
            pltpu.VMEM((NMO, count * TILE), jnp.bfloat16),
        ),
        in_specs=[hbm] * 4,
        out_specs=(vmem,) * 3,
        scratch_shapes=[
            pltpu.VMEM((count * SLOTS, TAU, TILE, TILE), jnp.bfloat16),
            pltpu.VMEM((count * SLOTS, TILE, TILE), jnp.bfloat16),
            pltpu.VMEM((count * TILE, NMO), jnp.bfloat16),
            pltpu.SMEM((count, SLOTS), jnp.int32),
            pltpu.SMEM((count * SLOTS + GROUP,), jnp.int32),
            pltpu.SemaphoreType.DMA((count * SLOTS, 2)),
            pltpu.SemaphoreType.DMA((2,)),
        ],
        compiler_params=pltpu.CompilerParams(vmem_limit_bytes=24 * MIB),
        cost_estimate=pl.CostEstimate(flops=2_000_000_000, bytes_accessed=12_000_000, transcendentals=0),
        name="tiles",
    )(*placed)


def beside(count, row, left, sigma, block):
    before, _, after = sides(count, row)
    slots = before if left else after
    if not slots:
        return None
    return contract(sigma, row, slots, block, row if left else row + slots[0] - BAND - count)


def project_kernel(count, split, piece, *refs):
    part, sigma, near, halo, transposed = refs[:5]
    outs, half = refs[5:-1], refs[-1]
    me = lax.axis_index("trow")
    first = lax.rem(me, 2) == 0
    columns = slice(piece * COLUMNS, (piece + 1) * COLUMNS)

    def finish(far_left):
        for row in range(count):
            value = part[row, :, columns]
            for left, block in ((not far_left, near), (far_left, halo)):
                term = beside(count, row, left, sigma, block)
                value = value if term is None else value + term
            for t in range(PAIRS):
                half[row * TILE : (row + 1) * TILE, t * COLUMNS : (t + 1) * COLUMNS] = value[
                    t * TILE : (t + 1) * TILE
                ].astype(jnp.bfloat16)

    @pl.when(first)
    def _():
        finish(True)

    @pl.when(jnp.logical_not(first))
    def _():
        finish(False)

    for k in range(NMO // TILE):
        block = lax.bitwise_xor(lax.div(me, 4), k) if split else k
        lhs = transposed[pl.ds(pl.multiple_of(block * TILE, TILE), TILE), :]
        total = jnp.dot(lhs, half[...], preferred_element_type=jnp.float32)
        if not split:
            outs[0][k * TILE : (k + 1) * TILE] = total
            continue
        keep, send = outs
        quarter = TILE // 4
        quarters = [total[q * quarter : (q + 1) * quarter] for q in range(4)]
        low_x = lax.rem(lax.div(me, 2), 2) == 0
        mine = [jnp.where(first, quarters[2 * x], quarters[2 * x + 1]) for x in range(2)]
        other = [jnp.where(first, quarters[2 * x + 1], quarters[2 * x]) for x in range(2)]
        for ref, pair in ((keep, mine), (send, other)):
            ref[2 * k] = jnp.where(low_x, pair[0], pair[1]).astype(ref.dtype)
            ref[2 * k + 1] = jnp.where(low_x, pair[1], pair[0]).astype(ref.dtype)


def project(part, sigma, near, halo, transposed, split, piece):
    count = part.shape[0]
    operands = (part, sigma, near, halo, transposed)
    vmem = pl.BlockSpec(memory_space=pltpu.VMEM)
    if split:
        shape = (8, NMO // 16, PAIRS * COLUMNS)
        out_shape = (pltpu.VMEM(shape, jnp.float32), pltpu.VMEM(shape, jnp.bfloat16))
    else:
        out_shape = (jax.ShapeDtypeStruct((NMO, PAIRS * COLUMNS), jnp.float32),)
    return pl.pallas_call(
        functools.partial(project_kernel, count, split, piece),
        out_shape=out_shape,
        in_specs=[vmem] * len(operands),
        out_specs=tuple(vmem for _ in out_shape),
        scratch_shapes=[pltpu.VMEM((count * TILE, PAIRS * COLUMNS), jnp.bfloat16)],
        compiler_params=pltpu.CompilerParams(vmem_limit_bytes=16 * MIB),
        cost_estimate=pl.CostEstimate(flops=800_000_000, bytes_accessed=3_000_000, transcendentals=0),
        name="project",
    )(*[pltpu.with_memory_space_constraint(x, pltpu.VMEM) for x in operands])


def freq_tables():
    point = np.arange(TAU, dtype=np.float32)
    freq = np.arange(NW, dtype=np.float32)
    pi = np.float32(np.pi)
    theta = pi * (np.float32(2.0) * point + np.float32(1.0)) / np.float32(2.0 * TAU)
    nodes = np.float32(0.5) * (np.float32(1.0) - np.cos(theta))
    weights = np.float32(np.pi / (2.0 * TAU)) * np.sin(theta)
    angle = pi * (np.float32(2.0) * freq[:, None] + np.float32(1.0)) * nodes[None, :]
    both = np.concatenate([weights[None, :] * np.cos(angle), weights[None, :] * np.sin(angle)], axis=0)
    folded = both[:, :PAIRS] + both[:, : PAIRS - 1 : -1]
    return folded.astype(np.float32).reshape(-1)


def frequency_kernel(terms, table, *refs):
    out, buffer, sems = refs[terms:]
    summed = refs[0][...]
    for ref in refs[1:terms]:
        summed = summed + ref[...].astype(jnp.float32)
    points = [
        jnp.concatenate(
            [summed[:, (piece * PAIRS + t) * COLUMNS : (piece * PAIRS + t + 1) * COLUMNS] for piece in range(CHUNKS)],
            axis=1,
        )
        for t in range(PAIRS)
    ]

    def copy(step):
        rows = pl.ds(step * FREQ_BLOCK, FREQ_BLOCK)
        return pltpu.make_async_copy(buffer.at[rows], out.at[rows], sems.at[step])

    @pl.loop(0, 2 * NW // FREQ_BLOCK)
    def _(step):
        @pl.loop(0, FREQ_BLOCK, unroll=4)
        def _(n):
            at = (step * FREQ_BLOCK + n) * PAIRS
            value = table[at] * points[0]
            for t in range(1, PAIRS):
                value = value + table[at + t] * points[t]
            buffer[step * FREQ_BLOCK + n] = value

        copy(step).start()

    @pl.loop(0, 2 * NW // FREQ_BLOCK)
    def _(step):
        copy(step).wait()


def frequency(*terms):
    rows = terms[0].shape[0]
    vmem = pl.BlockSpec(memory_space=pltpu.VMEM)
    out = pl.pallas_call(
        functools.partial(frequency_kernel, len(terms)),
        out_shape=jax.ShapeDtypeStruct((2 * NW, rows, NMO), jnp.float32),
        in_specs=[pl.BlockSpec(memory_space=pltpu.SMEM)] + [vmem] * len(terms),
        out_specs=pl.BlockSpec(memory_space=pl.ANY),
        scratch_shapes=[
            pltpu.VMEM((2 * NW, rows, NMO), jnp.float32),
            pltpu.SemaphoreType.DMA((2 * NW // FREQ_BLOCK,)),
        ],
        compiler_params=pltpu.CompilerParams(vmem_limit_bytes=24 * MIB),
        cost_estimate=pl.CostEstimate(flops=50_000_000, bytes_accessed=17_000_000, transcendentals=0),
        name="frequency",
    )(jnp.asarray(freq_tables()), *terms)
    return out.reshape(2, NW, rows, NMO)


def local(devices, green, integrals, pattern, coefficients):
    rows = coefficients.shape[0]
    width = BAND * TILE
    core = lax.rem(lax.axis_index("trow"), 2)
    partner = [(i, i ^ 1) for i in range(devices)]
    pairs = [(i, i + 1) for i in range(1, devices - 1, 2)]
    pairs += [(b, a) for a, b in pairs]
    halos, nears = [], []
    for piece in range(CHUNKS):
        away = lax.dynamic_slice(coefficients, (core * (rows - width), piece * COLUMNS), (width, COLUMNS))
        halos.append(lax.ppermute(away, "trow", pairs))
        inner = lax.dynamic_slice(coefficients, ((1 - core) * (rows - width), piece * COLUMNS), (width, COLUMNS))
        nears.append(lax.ppermute(inner, "trow", partner))
    part, sigma, transposed = tiles(green, integrals, pattern, coefficients)
    if devices != 16:
        summed = jnp.concatenate(
            [project(part, sigma, nears[piece], halos[piece], transposed, False, piece)[0] for piece in range(CHUNKS)], axis=1
        )
        return frequency(lax.psum_scatter(summed, "trow", scatter_dimension=0, tiled=True))
    keeps, arrived = [], []
    for piece in range(CHUNKS):
        keep, send = project(part, sigma, nears[piece], halos[piece], transposed, True, piece)
        keeps.append(keep)
        arrived.append(lax.ppermute(send, "trow", partner))
    sums = [
        jnp.concatenate([keep[k] + other[k].astype(jnp.float32) for keep, other in zip(keeps, arrived)], axis=1)
        for k in range(8)
    ]
    terms = [sums[0]]
    for k in (6, 7, 4, 5, 2, 3, 1):
        moves = [(i, i ^ (2 * k)) for i in range(devices)]
        terms.append(lax.ppermute(sums[k].astype(jnp.bfloat16), "trow", moves))
    return frequency(*terms)


def solution(mesh):
    in_specs = (
        P(("flake", "trow"), None, None, None, None),
        P(("flake", "trow"), None, None, None),
        P(("flake", "trow"), None),
        P(("flake", "trow"), None),
    )
    out_specs = P(None, None, ("flake", "trow"), None)
    return jax.shard_map(
        functools.partial(local, mesh.shape["trow"]),
        mesh=mesh,
        in_specs=in_specs,
        out_specs=out_specs,
        check_vma=False,
    )
```

```python
import functools

import jax
import jax.numpy as jnp
import numpy as np
from jax import lax
from jax.experimental import pallas as pl
from jax.experimental.pallas import tpu as pltpu
from jax.sharding import PartitionSpec as P

TILE = 128
BAND = 4
TAU = 4
PAIRS = TAU // 2
NMO = 512
NW = 128
SLOTS = 9
FREQ_BLOCK = 16
GROUP = 4
CHUNKS = 2
COLUMNS = NMO // CHUNKS
MIB = 1 << 20


def sides(count, row):
    return range(0, max(0, BAND - row)), range(max(0, BAND - row), min(SLOTS, count + BAND - row)), range(
        min(SLOTS, count + BAND - row), SLOTS
    )


def contract(sigma, row, slots, block, begin):
    lhs = jnp.concatenate([sigma[row, slot] for slot in slots], axis=1)
    rhs = block[begin * TILE : (begin + len(slots)) * TILE, :]
    return jnp.dot(lhs, rhs, preferred_element_type=jnp.float32)


def tiles_kernel(
    count,
    split,
    mask,
    green,
    integrals,
    coefficients,
    part,
    sigma,
    transposed,
    gbuf,
    ibuf,
    own,
    turned,
    pattern,
    order,
    sems,
    csem,
):
    def fetch(index):
        row, slot = index // SLOTS, index % SLOTS
        return (
            pltpu.make_async_copy(green.at[row, slot], gbuf.at[index], sems.at[index, 0]),
            pltpu.make_async_copy(integrals.at[row, slot], ibuf.at[index], sems.at[index, 1]),
        )

    def enlist(index, found):
        present = pattern[index // SLOTS, index % SLOTS] != 0

        @pl.when(present)
        def _():
            order[found] = index
            for copy in fetch(index):
                copy.start()

        return found + present.astype(jnp.int32)

    mask_copy = pltpu.make_async_copy(mask, pattern, csem.at[0])
    own_copy = pltpu.make_async_copy(coefficients, own, csem.at[1])
    mask_copy.start()
    own_copy.start()
    sigma[...] = jnp.zeros_like(sigma)
    mask_copy.wait()
    found = lax.fori_loop(0, count * SLOTS, enlist, jnp.int32(0))
    for extra in range(GROUP - 1):
        order[found + extra] = order[found - 1]
    own_copy.wait()
    for row in range(count):
        rows = slice(row * TILE, (row + 1) * TILE)
        (turned if split else transposed)[:, rows] = own[rows, :].T
    if split:
        place = lax.axis_index("trow")
        size = NMO // 16
        for k in range(16):
            owner = lax.bitwise_xor(place, 2 * (k % 8) + k // 8)
            transposed[k * size : (k + 1) * size, :] = turned[pl.ds(pl.multiple_of(owner * size, size), size), :]

    @pl.loop(0, pl.cdiv(found, GROUP))
    def _(group):
        indices = [order[group * GROUP + member] for member in range(GROUP)]
        for member, index in enumerate(indices):

            @pl.when(group * GROUP + member < found)
            def _():
                for copy in fetch(index):
                    copy.wait()

        for index in indices:
            paired = jnp.concatenate([gbuf[index, t] * gbuf[index, TAU - 1 - t] for t in range(PAIRS)], axis=0)
            product = jnp.dot(paired, ibuf[index], preferred_element_type=jnp.float32)
            sigma[index // SLOTS, index % SLOTS] = product.astype(jnp.bfloat16)

    for row in range(count):
        _, slots, _ = sides(count, row)
        part[row] = contract(sigma, row, slots, own, row + slots[0] - BAND)


def tiles(green, integrals, pattern, coefficients, split):
    count = green.shape[0]
    hbm = pl.BlockSpec(memory_space=pltpu.HBM)
    vmem = pl.BlockSpec(memory_space=pltpu.VMEM)
    placed = [pltpu.with_memory_space_constraint(x, pltpu.HBM) for x in (pattern, green, integrals, coefficients)]
    return pl.pallas_call(
        functools.partial(tiles_kernel, count, split),
        out_shape=(
            pltpu.VMEM((count, PAIRS * TILE, NMO), jnp.float32),
            pltpu.VMEM((count, SLOTS, PAIRS * TILE, TILE), jnp.bfloat16),
            pltpu.VMEM((NMO, count * TILE), jnp.bfloat16),
        ),
        in_specs=[hbm] * 4,
        out_specs=(vmem,) * 3,
        scratch_shapes=[
            pltpu.VMEM((count * SLOTS, TAU, TILE, TILE), jnp.bfloat16),
            pltpu.VMEM((count * SLOTS, TILE, TILE), jnp.bfloat16),
            pltpu.VMEM((count * TILE, NMO), jnp.bfloat16),
            pltpu.VMEM((NMO, count * TILE), jnp.bfloat16),
            pltpu.SMEM((count, SLOTS), jnp.int32),
            pltpu.SMEM((count * SLOTS + GROUP,), jnp.int32),
            pltpu.SemaphoreType.DMA((count * SLOTS, 2)),
            pltpu.SemaphoreType.DMA((2,)),
        ],
        compiler_params=pltpu.CompilerParams(vmem_limit_bytes=24 * MIB),
        cost_estimate=pl.CostEstimate(flops=2_000_000_000, bytes_accessed=12_000_000, transcendentals=0),
        name="tiles",
    )(*placed)


def outer(count, row, left, sigma, block):
    before, _, after = sides(count, row)
    slots = before if left else after
    if not slots:
        return None
    return contract(sigma, row, slots, block, row if left else row + slots[0] - BAND - count)


def project_kernel(count, split, piece, *refs):
    part, sigma, near, halo, transposed, out, half = refs
    first = lax.rem(lax.axis_index("trow"), 2) == 0
    columns = slice(piece * COLUMNS, (piece + 1) * COLUMNS)

    def finish(far_left):
        for row in range(count):
            value = part[row, :, columns]
            for left, block in ((not far_left, near), (far_left, halo)):
                term = outer(count, row, left, sigma, block)
                value = value if term is None else value + term
            for t in range(PAIRS):
                half[row * TILE : (row + 1) * TILE, t * COLUMNS : (t + 1) * COLUMNS] = value[
                    t * TILE : (t + 1) * TILE
                ].astype(jnp.bfloat16)

    @pl.when(first)
    def _():
        finish(True)

    @pl.when(jnp.logical_not(first))
    def _():
        finish(False)

    rows = slice(NMO // 2, NMO) if split else slice(0, NMO)
    out[...] = jnp.dot(transposed[rows, :], half[...], preferred_element_type=jnp.float32).astype(out.dtype)


def project(part, sigma, near, halo, transposed, split, piece):
    count = part.shape[0]
    operands = (part, sigma, near, halo, transposed)
    vmem = pl.BlockSpec(memory_space=pltpu.VMEM)
    if split:
        out_shape = pltpu.VMEM((NMO // 2, PAIRS * COLUMNS), jnp.bfloat16)
    else:
        out_shape = jax.ShapeDtypeStruct((NMO, PAIRS * COLUMNS), jnp.float32)
    return pl.pallas_call(
        functools.partial(project_kernel, count, split, piece),
        out_shape=(out_shape, pltpu.VMEM((count * TILE, PAIRS * COLUMNS), jnp.bfloat16)),
        in_specs=[vmem] * len(operands),
        out_specs=(vmem, vmem),
        compiler_params=pltpu.CompilerParams(vmem_limit_bytes=16 * MIB),
        cost_estimate=pl.CostEstimate(flops=500_000_000, bytes_accessed=3_000_000, transcendentals=0),
        name="project",
    )(*[pltpu.with_memory_space_constraint(x, pltpu.VMEM) for x in operands])


def keep_kernel(half, transposed, out):
    out[...] = jnp.dot(transposed[: NMO // 2, :], half[...], preferred_element_type=jnp.float32)


def project_own(half, transposed):
    vmem = pl.BlockSpec(memory_space=pltpu.VMEM)
    return pl.pallas_call(
        keep_kernel,
        out_shape=pltpu.VMEM((NMO // 2, half.shape[1]), jnp.float32),
        in_specs=[vmem, vmem],
        out_specs=vmem,
        compiler_params=pltpu.CompilerParams(vmem_limit_bytes=16 * MIB),
        cost_estimate=pl.CostEstimate(flops=400_000_000, bytes_accessed=2_000_000, transcendentals=0),
        name="project_own",
    )(*[pltpu.with_memory_space_constraint(x, pltpu.VMEM) for x in (half, transposed)])


def freq_tables():
    point = np.arange(TAU, dtype=np.float32)
    freq = np.arange(NW, dtype=np.float32)
    pi = np.float32(np.pi)
    theta = pi * (np.float32(2.0) * point + np.float32(1.0)) / np.float32(2.0 * TAU)
    nodes = np.float32(0.5) * (np.float32(1.0) - np.cos(theta))
    weights = np.float32(np.pi / (2.0 * TAU)) * np.sin(theta)
    angle = pi * (np.float32(2.0) * freq[:, None] + np.float32(1.0)) * nodes[None, :]
    both = np.concatenate([weights[None, :] * np.cos(angle), weights[None, :] * np.sin(angle)], axis=0)
    folded = both[:, :PAIRS] + both[:, : PAIRS - 1 : -1]
    return folded.astype(np.float32).reshape(-1)


def frequency_kernel(terms, table, *refs):
    out, buffer, sems = refs[terms:]
    summed = refs[0][...]
    for ref in refs[1:terms]:
        summed = summed + ref[...].astype(jnp.float32)
    points = [
        jnp.concatenate(
            [summed[:, (piece * PAIRS + t) * COLUMNS : (piece * PAIRS + t + 1) * COLUMNS] for piece in range(CHUNKS)],
            axis=1,
        )
        for t in range(PAIRS)
    ]

    def copy(step):
        rows = pl.ds(step * FREQ_BLOCK, FREQ_BLOCK)
        return pltpu.make_async_copy(buffer.at[rows], out.at[rows], sems.at[step])

    @pl.loop(0, 2 * NW // FREQ_BLOCK)
    def _(step):
        @pl.loop(0, FREQ_BLOCK, unroll=4)
        def _(n):
            at = (step * FREQ_BLOCK + n) * PAIRS
            value = table[at] * points[0]
            for t in range(1, PAIRS):
                value = value + table[at + t] * points[t]
            buffer[step * FREQ_BLOCK + n] = value

        copy(step).start()

    @pl.loop(0, 2 * NW // FREQ_BLOCK)
    def _(step):
        copy(step).wait()


def frequency(*terms):
    rows = terms[0].shape[0]
    vmem = pl.BlockSpec(memory_space=pltpu.VMEM)
    out = pl.pallas_call(
        functools.partial(frequency_kernel, len(terms)),
        out_shape=jax.ShapeDtypeStruct((2 * NW, rows, NMO), jnp.float32),
        in_specs=[pl.BlockSpec(memory_space=pltpu.SMEM)] + [vmem] * len(terms),
        out_specs=pl.BlockSpec(memory_space=pl.ANY),
        scratch_shapes=[
            pltpu.VMEM((2 * NW, rows, NMO), jnp.float32),
            pltpu.SemaphoreType.DMA((2 * NW // FREQ_BLOCK,)),
        ],
        compiler_params=pltpu.CompilerParams(vmem_limit_bytes=24 * MIB),
        cost_estimate=pl.CostEstimate(flops=50_000_000, bytes_accessed=17_000_000, transcendentals=0),
        name="frequency",
    )(jnp.asarray(freq_tables()), *terms)
    return out.reshape(2, NW, rows, NMO)


def local(devices, green, integrals, pattern, coefficients):
    rows = coefficients.shape[0]
    width = BAND * TILE
    core = lax.rem(lax.axis_index("trow"), 2)
    partner = [(i, i ^ 1) for i in range(devices)]
    pairs = [(i, i + 1) for i in range(1, devices - 1, 2)]
    pairs += [(b, a) for a, b in pairs]
    halos, nears = [], []
    for piece in range(CHUNKS):
        away = lax.dynamic_slice(coefficients, (core * (rows - width), piece * COLUMNS), (width, COLUMNS))
        halos.append(lax.ppermute(away, "trow", pairs))
        inner = lax.dynamic_slice(coefficients, ((1 - core) * (rows - width), piece * COLUMNS), (width, COLUMNS))
        nears.append(lax.ppermute(inner, "trow", partner))
    part, sigma, transposed = tiles(green, integrals, pattern, coefficients, devices == 16)
    if devices != 16:
        summed = jnp.concatenate(
            [project(part, sigma, nears[piece], halos[piece], transposed, False, piece)[0] for piece in range(CHUNKS)], axis=1
        )
        return frequency(lax.psum_scatter(summed, "trow", scatter_dimension=0, tiled=True))
    keeps, arrived = [], []
    for piece in range(CHUNKS):
        send, half = project(part, sigma, nears[piece], halos[piece], transposed, True, piece)
        arrived.append(lax.ppermute(send, "trow", partner))
        keeps.append(project_own(half, transposed))
    size = NMO // 16
    both = list(zip(keeps, arrived))
    sums = [
        jnp.concatenate(
            [keep[k * size : (k + 1) * size] + other[k * size : (k + 1) * size].astype(jnp.float32) for keep, other in both],
            axis=1,
        )
        for k in range(8)
    ]
    cast = [value.astype(jnp.bfloat16) for value in sums]
    flip = {k: [(i, i ^ (2 * k)) for i in range(devices)] for k in range(1, 8)}
    far = [lax.ppermute(cast[k], "trow", flip[k]) for k in (6, 7)]
    beside = lax.ppermute(jnp.stack([cast[1], cast[3]]), "trow", flip[1])
    far += [lax.ppermute(cast[k], "trow", flip[k]) for k in (4, 5)]
    onward = (sums[2] + beside[1].astype(jnp.float32)).astype(jnp.bfloat16)
    terms = [sums[0], beside[0]] + far + [lax.ppermute(onward, "trow", flip[2])]
    return frequency(*terms)


def solution(mesh):
    in_specs = (
        P(("flake", "trow"), None, None, None, None),
        P(("flake", "trow"), None, None, None),
        P(("flake", "trow"), None),
        P(("flake", "trow"), None),
    )
    out_specs = P(None, None, ("flake", "trow"), None)
    return jax.shard_map(
        functools.partial(local, mesh.shape["trow"]),
        mesh=mesh,
        in_specs=in_specs,
        out_specs=out_specs,
        check_vma=False,
    )
```

```python
import functools

import jax
import jax.numpy as jnp
import numpy as np
from jax import lax
from jax.experimental import pallas as pl
from jax.experimental.pallas import tpu as pltpu
from jax.sharding import PartitionSpec as P

TILE = 128
BAND = 4
TAU = 4
PAIRS = TAU // 2
NMO = 512
NW = 128
SLOTS = 9
FREQ_STEP = 4
FREQ_EDGES = [0, 2, 4, 8, 16, *range(32, 2 * NW + 1, 32)]
FREQ_BLOCKS = list(zip(FREQ_EDGES, FREQ_EDGES[1:]))
GROUP = 4
CHUNKS = 2
COLUMNS = NMO // CHUNKS
MIB = 1 << 20


def sides(count, row):
    return range(0, max(0, BAND - row)), range(max(0, BAND - row), min(SLOTS, count + BAND - row)), range(
        min(SLOTS, count + BAND - row), SLOTS
    )


def contract(sigma, row, slots, block, begin):
    lhs = jnp.concatenate([sigma[row, slot] for slot in slots], axis=1)
    rhs = block[begin * TILE : (begin + len(slots)) * TILE, :]
    return jnp.dot(lhs, rhs, preferred_element_type=jnp.float32)


def tiles_kernel(
    count,
    split,
    mask,
    green,
    integrals,
    coefficients,
    part,
    sigma,
    transposed,
    gbuf,
    ibuf,
    own,
    turned,
    pattern,
    order,
    sems,
    csem,
):
    def fetch(index):
        row, slot = index // SLOTS, index % SLOTS
        return (
            pltpu.make_async_copy(green.at[row, slot], gbuf.at[index], sems.at[index, 0]),
            pltpu.make_async_copy(integrals.at[row, slot], ibuf.at[index], sems.at[index, 1]),
        )

    def enlist(index, found):
        present = pattern[index // SLOTS, index % SLOTS] != 0

        @pl.when(present)
        def _():
            order[found] = index
            for copy in fetch(index):
                copy.start()

        return found + present.astype(jnp.int32)

    mask_copy = pltpu.make_async_copy(mask, pattern, csem.at[0])
    own_copy = pltpu.make_async_copy(coefficients, own, csem.at[1])
    mask_copy.start()
    own_copy.start()
    sigma[...] = jnp.zeros_like(sigma)
    mask_copy.wait()
    found = lax.fori_loop(0, count * SLOTS, enlist, jnp.int32(0))
    for extra in range(GROUP - 1):
        order[found + extra] = order[found - 1]
    own_copy.wait()
    for row in range(count):
        rows = slice(row * TILE, (row + 1) * TILE)
        (turned if split else transposed)[:, rows] = own[rows, :].T
    if split:
        place = lax.axis_index("trow")
        size = NMO // 16
        for k in range(16):
            owner = lax.bitwise_xor(place, 2 * (k % 8) + k // 8)
            transposed[k * size : (k + 1) * size, :] = turned[pl.ds(pl.multiple_of(owner * size, size), size), :]

    @pl.loop(0, pl.cdiv(found, GROUP))
    def _(group):
        indices = [order[group * GROUP + member] for member in range(GROUP)]
        for member, index in enumerate(indices):

            @pl.when(group * GROUP + member < found)
            def _():
                for copy in fetch(index):
                    copy.wait()

        for index in indices:
            paired = jnp.concatenate([gbuf[index, t] * gbuf[index, TAU - 1 - t] for t in range(PAIRS)], axis=0)
            product = jnp.dot(paired, ibuf[index], preferred_element_type=jnp.float32)
            sigma[index // SLOTS, index % SLOTS] = product.astype(jnp.bfloat16)

    for row in range(count):
        _, slots, _ = sides(count, row)
        part[row] = contract(sigma, row, slots, own, row + slots[0] - BAND)


def tiles(green, integrals, pattern, coefficients, split):
    count = green.shape[0]
    hbm = pl.BlockSpec(memory_space=pltpu.HBM)
    vmem = pl.BlockSpec(memory_space=pltpu.VMEM)
    placed = [pltpu.with_memory_space_constraint(x, pltpu.HBM) for x in (pattern, green, integrals, coefficients)]
    return pl.pallas_call(
        functools.partial(tiles_kernel, count, split),
        out_shape=(
            pltpu.VMEM((count, PAIRS * TILE, NMO), jnp.float32),
            pltpu.VMEM((count, SLOTS, PAIRS * TILE, TILE), jnp.bfloat16),
            pltpu.VMEM((NMO, count * TILE), jnp.bfloat16),
        ),
        in_specs=[hbm] * 4,
        out_specs=(vmem,) * 3,
        scratch_shapes=[
            pltpu.VMEM((count * SLOTS, TAU, TILE, TILE), jnp.bfloat16),
            pltpu.VMEM((count * SLOTS, TILE, TILE), jnp.bfloat16),
            pltpu.VMEM((count * TILE, NMO), jnp.bfloat16),
            pltpu.VMEM((NMO, count * TILE), jnp.bfloat16),
            pltpu.SMEM((count, SLOTS), jnp.int32),
            pltpu.SMEM((count * SLOTS + GROUP,), jnp.int32),
            pltpu.SemaphoreType.DMA((count * SLOTS, 2)),
            pltpu.SemaphoreType.DMA((2,)),
        ],
        compiler_params=pltpu.CompilerParams(vmem_limit_bytes=24 * MIB),
        cost_estimate=pl.CostEstimate(flops=2_000_000_000, bytes_accessed=12_000_000, transcendentals=0),
        name="tiles",
    )(*placed)


def outer(count, row, left, sigma, block):
    before, _, after = sides(count, row)
    slots = before if left else after
    if not slots:
        return None
    return contract(sigma, row, slots, block, row if left else row + slots[0] - BAND - count)


def project_kernel(count, split, piece, *refs):
    part, sigma, near, halo, transposed, out, half = refs
    first = lax.rem(lax.axis_index("trow"), 2) == 0
    columns = slice(piece * COLUMNS, (piece + 1) * COLUMNS)

    def finish(far_left):
        for row in range(count):
            value = part[row, :, columns]
            for left, block in ((not far_left, near), (far_left, halo)):
                term = outer(count, row, left, sigma, block)
                value = value if term is None else value + term
            for t in range(PAIRS):
                half[row * TILE : (row + 1) * TILE, t * COLUMNS : (t + 1) * COLUMNS] = value[
                    t * TILE : (t + 1) * TILE
                ].astype(jnp.bfloat16)

    @pl.when(first)
    def _():
        finish(True)

    @pl.when(jnp.logical_not(first))
    def _():
        finish(False)

    rows = slice(NMO // 2, NMO) if split else slice(0, NMO)
    out[...] = jnp.dot(transposed[rows, :], half[...], preferred_element_type=jnp.float32).astype(out.dtype)


def project(part, sigma, near, halo, transposed, split, piece):
    count = part.shape[0]
    operands = (part, sigma, near, halo, transposed)
    vmem = pl.BlockSpec(memory_space=pltpu.VMEM)
    if split:
        out_shape = pltpu.VMEM((NMO // 2, PAIRS * COLUMNS), jnp.bfloat16)
    else:
        out_shape = jax.ShapeDtypeStruct((NMO, PAIRS * COLUMNS), jnp.float32)
    return pl.pallas_call(
        functools.partial(project_kernel, count, split, piece),
        out_shape=(out_shape, pltpu.VMEM((count * TILE, PAIRS * COLUMNS), jnp.bfloat16)),
        in_specs=[vmem] * len(operands),
        out_specs=(vmem, vmem),
        compiler_params=pltpu.CompilerParams(vmem_limit_bytes=16 * MIB),
        cost_estimate=pl.CostEstimate(flops=500_000_000, bytes_accessed=3_000_000, transcendentals=0),
        name="project",
    )(*[pltpu.with_memory_space_constraint(x, pltpu.VMEM) for x in operands])


def keep_kernel(half, transposed, out):
    out[...] = jnp.dot(transposed[: NMO // 2, :], half[...], preferred_element_type=jnp.float32)


def project_own(half, transposed):
    vmem = pl.BlockSpec(memory_space=pltpu.VMEM)
    return pl.pallas_call(
        keep_kernel,
        out_shape=pltpu.VMEM((NMO // 2, half.shape[1]), jnp.float32),
        in_specs=[vmem, vmem],
        out_specs=vmem,
        compiler_params=pltpu.CompilerParams(vmem_limit_bytes=16 * MIB),
        cost_estimate=pl.CostEstimate(flops=400_000_000, bytes_accessed=2_000_000, transcendentals=0),
        name="project_own",
    )(*[pltpu.with_memory_space_constraint(x, pltpu.VMEM) for x in (half, transposed)])


def freq_tables():
    point = np.arange(TAU, dtype=np.float32)
    freq = np.arange(NW, dtype=np.float32)
    pi = np.float32(np.pi)
    theta = pi * (np.float32(2.0) * point + np.float32(1.0)) / np.float32(2.0 * TAU)
    nodes = np.float32(0.5) * (np.float32(1.0) - np.cos(theta))
    weights = np.float32(np.pi / (2.0 * TAU)) * np.sin(theta)
    angle = pi * (np.float32(2.0) * freq[:, None] + np.float32(1.0)) * nodes[None, :]
    both = np.concatenate([weights[None, :] * np.cos(angle), weights[None, :] * np.sin(angle)], axis=0)
    folded = both[:, :PAIRS] + both[:, : PAIRS - 1 : -1]
    return np.repeat(folded.astype(np.float32).reshape(-1, 1), TILE, axis=1)


def frequency_kernel(terms, table, *refs):
    out, buffer, sems = refs[terms:]
    summed = refs[0][...]
    for ref in refs[1:terms]:
        summed = summed + ref[...].astype(jnp.float32)
    points = [
        jnp.concatenate(
            [summed[:, (piece * PAIRS + t) * COLUMNS : (piece * PAIRS + t + 1) * COLUMNS] for piece in range(CHUNKS)],
            axis=1,
        )
        for t in range(PAIRS)
    ]

    def number(at):
        return jnp.concatenate([table[pl.ds(at, 1), :]] * (NMO // TILE), axis=1)

    def transform(n):
        value = number(n * PAIRS) * points[0]
        for t in range(1, PAIRS):
            value = value + number(n * PAIRS + t) * points[t]
        buffer[n] = value

    copies = []
    for index, (begin, end) in enumerate(FREQ_BLOCKS):
        if end - begin <= FREQ_STEP:
            for n in range(begin, end):
                transform(n)
        else:
            pl.loop(begin, end, unroll=FREQ_STEP)(transform)
        copies.append(pltpu.make_async_copy(buffer.at[begin:end], out.at[begin:end], sems.at[index]))
        copies[-1].start()
    for copy in copies:
        copy.wait()


def frequency(*terms):
    rows = terms[0].shape[0]
    vmem = pl.BlockSpec(memory_space=pltpu.VMEM)
    out = pl.pallas_call(
        functools.partial(frequency_kernel, len(terms)),
        out_shape=jax.ShapeDtypeStruct((2 * NW, rows, NMO), jnp.float32),
        in_specs=[vmem] * (1 + len(terms)),
        out_specs=pl.BlockSpec(memory_space=pl.ANY),
        scratch_shapes=[
            pltpu.VMEM((2 * NW, rows, NMO), jnp.float32),
            pltpu.SemaphoreType.DMA((len(FREQ_BLOCKS),)),
        ],
        compiler_params=pltpu.CompilerParams(vmem_limit_bytes=24 * MIB),
        cost_estimate=pl.CostEstimate(flops=50_000_000, bytes_accessed=17_000_000, transcendentals=0),
        name="frequency",
    )(*[pltpu.with_memory_space_constraint(x, pltpu.VMEM) for x in (jnp.asarray(freq_tables()), *terms)])
    return out.reshape(2, NW, rows, NMO)


def local(devices, green, integrals, pattern, coefficients):
    rows = coefficients.shape[0]
    width = BAND * TILE
    core = lax.rem(lax.axis_index("trow"), 2)
    partner = [(i, i ^ 1) for i in range(devices)]
    pairs = [(i, i + 1) for i in range(1, devices - 1, 2)]
    pairs += [(b, a) for a, b in pairs]
    halos, nears = [], []
    for piece in range(CHUNKS):
        away = lax.dynamic_slice(coefficients, (core * (rows - width), piece * COLUMNS), (width, COLUMNS))
        halos.append(lax.ppermute(away, "trow", pairs))
        inner = lax.dynamic_slice(coefficients, ((1 - core) * (rows - width), piece * COLUMNS), (width, COLUMNS))
        nears.append(lax.ppermute(inner, "trow", partner))
    part, sigma, transposed = tiles(green, integrals, pattern, coefficients, devices == 16)
    if devices != 16:
        summed = jnp.concatenate(
            [project(part, sigma, nears[piece], halos[piece], transposed, False, piece)[0] for piece in range(CHUNKS)], axis=1
        )
        return frequency(lax.psum_scatter(summed, "trow", scatter_dimension=0, tiled=True))
    keeps, arrived = [], []
    for piece in range(CHUNKS):
        send, half = project(part, sigma, nears[piece], halos[piece], transposed, True, piece)
        arrived.append(lax.ppermute(send, "trow", partner))
        keeps.append(project_own(half, transposed))
    size = NMO // 16
    both = list(zip(keeps, arrived))
    sums = [
        jnp.concatenate(
            [keep[k * size : (k + 1) * size] + other[k * size : (k + 1) * size].astype(jnp.float32) for keep, other in both],
            axis=1,
        )
        for k in range(8)
    ]
    cast = [value.astype(jnp.bfloat16) for value in sums]
    flip = {k: [(i, i ^ (2 * k)) for i in range(devices)] for k in range(1, 8)}
    beside = lax.ppermute(jnp.stack([cast[k] for k in (1, 3, 7)]), "trow", flip[1])
    straight = {k: lax.ppermute(cast[k], "trow", flip[k]) for k in (4, 5)}
    own = sums[0] + beside[0].astype(jnp.float32)
    merged = {k: lax.ppermute((sums[k] + beside[at].astype(jnp.float32)).astype(jnp.bfloat16), "trow", flip[k]) for at, k in ((1, 2), (2, 6))}
    terms = [own] + [straight[k] for k in (4, 5)] + [merged[k] for k in (2, 6)]
    return frequency(*terms)


def solution(mesh):
    in_specs = (
        P(("flake", "trow"), None, None, None, None),
        P(("flake", "trow"), None, None, None),
        P(("flake", "trow"), None),
        P(("flake", "trow"), None),
    )
    out_specs = P(None, None, ("flake", "trow"), None)
    return jax.shard_map(
        functools.partial(local, mesh.shape["trow"]),
        mesh=mesh,
        in_specs=in_specs,
        out_specs=out_specs,
        check_vma=False,
    )
```

```python
import functools

import jax
import jax.numpy as jnp
import numpy as np
from jax import lax
from jax.experimental import pallas as pl
from jax.experimental.pallas import tpu as pltpu
from jax.sharding import PartitionSpec as P

TILE = 128
BAND = 4
TAU = 4
PAIRS = TAU // 2
NMO = 512
NW = 128
SLOTS = 9
FREQ_STEP = 4
FREQ_EDGES = [0, 2, 4, 8, 16, *range(32, 2 * NW + 1, 32)]
FREQ_BLOCKS = list(zip(FREQ_EDGES, FREQ_EDGES[1:]))
GROUP = 4
CHUNKS = 2
COLUMNS = NMO // CHUNKS
MIB = 1 << 20


def sides(count, row):
    return range(0, max(0, BAND - row)), range(max(0, BAND - row), min(SLOTS, count + BAND - row)), range(
        min(SLOTS, count + BAND - row), SLOTS
    )


def contract(sigma, row, slots, block, begin):
    lhs = jnp.concatenate([sigma[row, slot] for slot in slots], axis=1)
    rhs = block[begin * TILE : (begin + len(slots)) * TILE, :]
    return jnp.dot(lhs, rhs, preferred_element_type=jnp.float32)


def tiles_kernel(
    count,
    split,
    mask,
    green,
    integrals,
    coefficients,
    part,
    sigma,
    transposed,
    gbuf,
    ibuf,
    own,
    turned,
    pattern,
    order,
    sems,
    csem,
):
    def fetch(index):
        row, slot = index // SLOTS, index % SLOTS
        return (
            pltpu.make_async_copy(green.at[row, slot], gbuf.at[index], sems.at[index, 0]),
            pltpu.make_async_copy(integrals.at[row, slot], ibuf.at[index], sems.at[index, 1]),
        )

    def enlist(index, found):
        present = pattern[index // SLOTS, index % SLOTS] != 0

        @pl.when(present)
        def _():
            order[found] = index
            for copy in fetch(index):
                copy.start()

        return found + present.astype(jnp.int32)

    mask_copy = pltpu.make_async_copy(mask, pattern, csem.at[0])
    own_copy = pltpu.make_async_copy(coefficients, own, csem.at[1])
    mask_copy.start()
    own_copy.start()
    sigma[...] = jnp.zeros_like(sigma)
    mask_copy.wait()
    found = lax.fori_loop(0, count * SLOTS, enlist, jnp.int32(0))
    for extra in range(GROUP - 1):
        order[found + extra] = order[found - 1]
    own_copy.wait()
    for row in range(count):
        rows = slice(row * TILE, (row + 1) * TILE)
        (turned if split else transposed)[:, rows] = own[rows, :].T
    if split:
        place = lax.axis_index("trow")
        size = NMO // 16
        for k in range(16):
            owner = lax.bitwise_xor(place, 2 * (k % 8) + k // 8)
            transposed[k * size : (k + 1) * size, :] = turned[pl.ds(pl.multiple_of(owner * size, size), size), :]

    @pl.loop(0, pl.cdiv(found, GROUP))
    def _(group):
        indices = [order[group * GROUP + member] for member in range(GROUP)]
        for member, index in enumerate(indices):

            @pl.when(group * GROUP + member < found)
            def _():
                for copy in fetch(index):
                    copy.wait()

        for index in indices:
            paired = jnp.concatenate([gbuf[index, t] * gbuf[index, TAU - 1 - t] for t in range(PAIRS)], axis=0)
            product = jnp.dot(paired, ibuf[index], preferred_element_type=jnp.float32)
            sigma[index // SLOTS, index % SLOTS] = product.astype(jnp.bfloat16)

    for row in range(count):
        _, slots, _ = sides(count, row)
        part[row] = contract(sigma, row, slots, own, row + slots[0] - BAND)


def tiles(green, integrals, pattern, coefficients, split):
    count = green.shape[0]
    hbm = pl.BlockSpec(memory_space=pltpu.HBM)
    vmem = pl.BlockSpec(memory_space=pltpu.VMEM)
    placed = [pltpu.with_memory_space_constraint(x, pltpu.HBM) for x in (pattern, green, integrals, coefficients)]
    return pl.pallas_call(
        functools.partial(tiles_kernel, count, split),
        out_shape=(
            pltpu.VMEM((count, PAIRS * TILE, NMO), jnp.float32),
            pltpu.VMEM((count, SLOTS, PAIRS * TILE, TILE), jnp.bfloat16),
            pltpu.VMEM((NMO, count * TILE), jnp.bfloat16),
        ),
        in_specs=[hbm] * 4,
        out_specs=(vmem,) * 3,
        scratch_shapes=[
            pltpu.VMEM((count * SLOTS, TAU, TILE, TILE), jnp.bfloat16),
            pltpu.VMEM((count * SLOTS, TILE, TILE), jnp.bfloat16),
            pltpu.VMEM((count * TILE, NMO), jnp.bfloat16),
            pltpu.VMEM((NMO, count * TILE), jnp.bfloat16),
            pltpu.SMEM((count, SLOTS), jnp.int32),
            pltpu.SMEM((count * SLOTS + GROUP,), jnp.int32),
            pltpu.SemaphoreType.DMA((count * SLOTS, 2)),
            pltpu.SemaphoreType.DMA((2,)),
        ],
        compiler_params=pltpu.CompilerParams(vmem_limit_bytes=24 * MIB),
        cost_estimate=pl.CostEstimate(flops=2_000_000_000, bytes_accessed=12_000_000, transcendentals=0),
        name="tiles",
    )(*placed)


def outer(count, row, left, sigma, block):
    before, _, after = sides(count, row)
    slots = before if left else after
    if not slots:
        return None
    return contract(sigma, row, slots, block, row if left else row + slots[0] - BAND - count)


def project_kernel(count, split, piece, *refs):
    part, sigma, near, halo, transposed, out, half = refs
    first = lax.rem(lax.axis_index("trow"), 2) == 0
    columns = slice(piece * COLUMNS, (piece + 1) * COLUMNS)

    def finish(far_left):
        for row in range(count):
            value = part[row, :, columns]
            for left, block in ((not far_left, near), (far_left, halo)):
                term = outer(count, row, left, sigma, block)
                value = value if term is None else value + term
            for t in range(PAIRS):
                half[row * TILE : (row + 1) * TILE, t * COLUMNS : (t + 1) * COLUMNS] = value[
                    t * TILE : (t + 1) * TILE
                ].astype(jnp.bfloat16)

    @pl.when(first)
    def _():
        finish(True)

    @pl.when(jnp.logical_not(first))
    def _():
        finish(False)

    rows = slice(NMO // 2, NMO) if split else slice(0, NMO)
    out[...] = jnp.dot(transposed[rows, :], half[...], preferred_element_type=jnp.float32).astype(out.dtype)


def project(part, sigma, near, halo, transposed, split, piece):
    count = part.shape[0]
    operands = (part, sigma, near, halo, transposed)
    vmem = pl.BlockSpec(memory_space=pltpu.VMEM)
    if split:
        out_shape = pltpu.VMEM((NMO // 2, PAIRS * COLUMNS), jnp.bfloat16)
    else:
        out_shape = jax.ShapeDtypeStruct((NMO, PAIRS * COLUMNS), jnp.float32)
    return pl.pallas_call(
        functools.partial(project_kernel, count, split, piece),
        out_shape=(out_shape, pltpu.VMEM((count * TILE, PAIRS * COLUMNS), jnp.bfloat16)),
        in_specs=[vmem] * len(operands),
        out_specs=(vmem, vmem),
        compiler_params=pltpu.CompilerParams(vmem_limit_bytes=16 * MIB),
        cost_estimate=pl.CostEstimate(flops=500_000_000, bytes_accessed=3_000_000, transcendentals=0),
        name="project",
    )(*[pltpu.with_memory_space_constraint(x, pltpu.VMEM) for x in operands])


def keep_kernel(half, transposed, out):
    out[...] = jnp.dot(transposed[: NMO // 2, :], half[...], preferred_element_type=jnp.float32)


def project_own(half, transposed):
    vmem = pl.BlockSpec(memory_space=pltpu.VMEM)
    return pl.pallas_call(
        keep_kernel,
        out_shape=pltpu.VMEM((NMO // 2, half.shape[1]), jnp.float32),
        in_specs=[vmem, vmem],
        out_specs=vmem,
        compiler_params=pltpu.CompilerParams(vmem_limit_bytes=16 * MIB),
        cost_estimate=pl.CostEstimate(flops=400_000_000, bytes_accessed=2_000_000, transcendentals=0),
        name="project_own",
    )(*[pltpu.with_memory_space_constraint(x, pltpu.VMEM) for x in (half, transposed)])


def freq_tables():
    point = np.arange(TAU, dtype=np.float32)
    freq = np.arange(NW, dtype=np.float32)
    pi = np.float32(np.pi)
    theta = pi * (np.float32(2.0) * point + np.float32(1.0)) / np.float32(2.0 * TAU)
    nodes = np.float32(0.5) * (np.float32(1.0) - np.cos(theta))
    weights = np.float32(np.pi / (2.0 * TAU)) * np.sin(theta)
    angle = pi * (np.float32(2.0) * freq[:, None] + np.float32(1.0)) * nodes[None, :]
    both = np.concatenate([weights[None, :] * np.cos(angle), weights[None, :] * np.sin(angle)], axis=0)
    folded = both[:, :PAIRS] + both[:, : PAIRS - 1 : -1]
    return np.repeat(folded.astype(np.float32).reshape(-1, 1), TILE, axis=1)


def frequency_kernel(terms, table, *refs):
    out, buffer, sems = refs[terms:]
    summed = refs[0][...]
    for ref in refs[1:terms]:
        summed = summed + ref[...].astype(jnp.float32)
    points = [
        jnp.concatenate(
            [summed[:, (piece * PAIRS + t) * COLUMNS : (piece * PAIRS + t + 1) * COLUMNS] for piece in range(CHUNKS)],
            axis=1,
        )
        for t in range(PAIRS)
    ]

    def number(at):
        return jnp.concatenate([table[pl.ds(at, 1), :]] * (NMO // TILE), axis=1)

    def transform(n):
        value = number(n * PAIRS) * points[0]
        for t in range(1, PAIRS):
            value = value + number(n * PAIRS + t) * points[t]
        buffer[n] = value

    copies = []
    for index, (begin, end) in enumerate(FREQ_BLOCKS):
        if end - begin <= FREQ_STEP:
            for n in range(begin, end):
                transform(n)
        else:
            pl.loop(begin, end, unroll=FREQ_STEP)(transform)
        copies.append(pltpu.make_async_copy(buffer.at[begin:end], out.at[begin:end], sems.at[index]))
        copies[-1].start()
    for copy in copies:
        copy.wait()


def frequency(*terms):
    rows = terms[0].shape[0]
    vmem = pl.BlockSpec(memory_space=pltpu.VMEM)
    out = pl.pallas_call(
        functools.partial(frequency_kernel, len(terms)),
        out_shape=jax.ShapeDtypeStruct((2 * NW, rows, NMO), jnp.float32),
        in_specs=[vmem] * (1 + len(terms)),
        out_specs=pl.BlockSpec(memory_space=pl.ANY),
        scratch_shapes=[
            pltpu.VMEM((2 * NW, rows, NMO), jnp.float32),
            pltpu.SemaphoreType.DMA((len(FREQ_BLOCKS),)),
        ],
        compiler_params=pltpu.CompilerParams(vmem_limit_bytes=24 * MIB),
        cost_estimate=pl.CostEstimate(flops=50_000_000, bytes_accessed=17_000_000, transcendentals=0),
        name="frequency",
    )(*[pltpu.with_memory_space_constraint(x, pltpu.VMEM) for x in (jnp.asarray(freq_tables()), *terms)])
    return out.reshape(2, NW, rows, NMO)


def local(devices, green, integrals, pattern, coefficients):
    rows = coefficients.shape[0]
    width = BAND * TILE
    core = lax.rem(lax.axis_index("trow"), 2)
    partner = [(i, i ^ 1) for i in range(devices)]
    pairs = [(i, i + 1) for i in range(1, devices - 1, 2)]
    pairs += [(b, a) for a, b in pairs]
    halos, nears = [], []
    for piece in range(CHUNKS):
        away = lax.dynamic_slice(coefficients, (core * (rows - width), piece * COLUMNS), (width, COLUMNS))
        halos.append(lax.ppermute(away, "trow", pairs))
        inner = lax.dynamic_slice(coefficients, ((1 - core) * (rows - width), piece * COLUMNS), (width, COLUMNS))
        nears.append(lax.ppermute(inner, "trow", partner))
    part, sigma, transposed = tiles(green, integrals, pattern, coefficients, devices == 16)
    if devices != 16:
        summed = jnp.concatenate(
            [project(part, sigma, nears[piece], halos[piece], transposed, False, piece)[0] for piece in range(CHUNKS)], axis=1
        )
        return frequency(lax.psum_scatter(summed, "trow", scatter_dimension=0, tiled=True))
    keeps, arrived = [], []
    for piece in range(CHUNKS):
        send, half = project(part, sigma, nears[piece], halos[piece], transposed, True, piece)
        arrived.append(lax.ppermute(send, "trow", partner))
        keeps.append(project_own(half, transposed))
    size = NMO // 16
    both = list(zip(keeps, arrived))
    sums = [
        jnp.concatenate(
            [keep[k * size : (k + 1) * size] + other[k * size : (k + 1) * size].astype(jnp.float32) for keep, other in both],
            axis=1,
        )
        for k in range(8)
    ]
    cast = [value.astype(jnp.bfloat16) for value in sums]
    flip = {k: [(i, i ^ (2 * k)) for i in range(devices)] for k in range(1, 8)}
    parts = []
    for keep, other in both:
        blocks = [
            keep[k * size : (k + 1) * size] + other[k * size : (k + 1) * size].astype(jnp.float32) for k in (1, 3, 5)
        ]
        parts.append(lax.ppermute(jnp.stack(blocks).astype(jnp.bfloat16), "trow", flip[1]))
    beside = jnp.concatenate(lax.optimization_barrier(parts), axis=2).astype(jnp.float32)
    straight = [lax.ppermute(cast[k], "trow", flip[k]) for k in (6, 7)]
    merged = [
        lax.ppermute((sums[k] + beside[at]).astype(jnp.bfloat16), "trow", flip[k]) for at, k in ((1, 2), (2, 4))
    ]
    terms = [sums[0] + beside[0], *straight, *merged]
    return frequency(*terms)


def solution(mesh):
    in_specs = (
        P(("flake", "trow"), None, None, None, None),
        P(("flake", "trow"), None, None, None),
        P(("flake", "trow"), None),
        P(("flake", "trow"), None),
    )
    out_specs = P(None, None, ("flake", "trow"), None)
    return jax.shard_map(
        functools.partial(local, mesh.shape["trow"]),
        mesh=mesh,
        in_specs=in_specs,
        out_specs=out_specs,
        check_vma=False,
    )
```

```python
import functools

import jax
import jax.numpy as jnp
import numpy as np
from jax import lax
from jax.experimental import pallas as pl
from jax.experimental.pallas import tpu as pltpu
from jax.sharding import PartitionSpec as P

TILE = 128
BAND = 4
TAU = 4
PAIRS = TAU // 2
NMO = 512
NW = 128
SLOTS = 9
FREQ_STEP = 4
FREQ_EDGES = [0, 2, 4, 8, 16, *range(32, 2 * NW + 1, 32)]
FREQ_BLOCKS = list(zip(FREQ_EDGES, FREQ_EDGES[1:]))
GROUP = 4
CHUNKS = 2
COLUMNS = NMO // CHUNKS
MIB = 1 << 20


def sides(count, row):
    return range(0, max(0, BAND - row)), range(max(0, BAND - row), min(SLOTS, count + BAND - row)), range(
        min(SLOTS, count + BAND - row), SLOTS
    )


def contract(sigma, row, slots, block, begin):
    lhs = jnp.concatenate([sigma[row, slot] for slot in slots], axis=1)
    rhs = block[begin * TILE : (begin + len(slots)) * TILE, :]
    return jnp.dot(lhs, rhs, preferred_element_type=jnp.float32)


def tiles_kernel(
    count,
    split,
    mask,
    green,
    integrals,
    coefficients,
    part,
    sigma,
    transposed,
    gbuf,
    ibuf,
    own,
    turned,
    pattern,
    order,
    sems,
    csem,
):
    def fetch(index):
        row, slot = index // SLOTS, index % SLOTS
        return (
            pltpu.make_async_copy(green.at[row, slot], gbuf.at[index], sems.at[index, 0]),
            pltpu.make_async_copy(integrals.at[row, slot], ibuf.at[index], sems.at[index, 1]),
        )

    def enlist(index, found):
        present = pattern[index // SLOTS, index % SLOTS] != 0

        @pl.when(present)
        def _():
            order[found] = index
            for copy in fetch(index):
                copy.start()

        return found + present.astype(jnp.int32)

    mask_copy = pltpu.make_async_copy(mask, pattern, csem.at[0])
    own_copy = pltpu.make_async_copy(coefficients, own, csem.at[1])
    mask_copy.start()
    own_copy.start()
    sigma[...] = jnp.zeros_like(sigma)
    mask_copy.wait()
    found = lax.fori_loop(0, count * SLOTS, enlist, jnp.int32(0))
    for extra in range(GROUP - 1):
        order[found + extra] = order[found - 1]
    own_copy.wait()
    for row in range(count):
        rows = slice(row * TILE, (row + 1) * TILE)
        (turned if split else transposed)[:, rows] = own[rows, :].T
    if split:
        place = lax.axis_index("trow")
        size = NMO // 16
        for k in range(16):
            owner = lax.bitwise_xor(place, 2 * (k % 8) + k // 8)
            transposed[k * size : (k + 1) * size, :] = turned[pl.ds(pl.multiple_of(owner * size, size), size), :]

    @pl.loop(0, pl.cdiv(found, GROUP))
    def _(group):
        indices = [order[group * GROUP + member] for member in range(GROUP)]
        for member, index in enumerate(indices):

            @pl.when(group * GROUP + member < found)
            def _():
                for copy in fetch(index):
                    copy.wait()

        for index in indices:
            paired = jnp.concatenate([gbuf[index, t] * gbuf[index, TAU - 1 - t] for t in range(PAIRS)], axis=0)
            product = jnp.dot(paired, ibuf[index], preferred_element_type=jnp.float32)
            sigma[index // SLOTS, index % SLOTS] = product.astype(jnp.bfloat16)

    for row in range(count):
        _, slots, _ = sides(count, row)
        part[row] = contract(sigma, row, slots, own, row + slots[0] - BAND)


def tiles(green, integrals, pattern, coefficients, split):
    count = green.shape[0]
    hbm = pl.BlockSpec(memory_space=pltpu.HBM)
    vmem = pl.BlockSpec(memory_space=pltpu.VMEM)
    placed = [pltpu.with_memory_space_constraint(x, pltpu.HBM) for x in (pattern, green, integrals, coefficients)]
    return pl.pallas_call(
        functools.partial(tiles_kernel, count, split),
        out_shape=(
            pltpu.VMEM((count, PAIRS * TILE, NMO), jnp.float32),
            pltpu.VMEM((count, SLOTS, PAIRS * TILE, TILE), jnp.bfloat16),
            pltpu.VMEM((NMO, count * TILE), jnp.bfloat16),
        ),
        in_specs=[hbm] * 4,
        out_specs=(vmem,) * 3,
        scratch_shapes=[
            pltpu.VMEM((count * SLOTS, TAU, TILE, TILE), jnp.bfloat16),
            pltpu.VMEM((count * SLOTS, TILE, TILE), jnp.bfloat16),
            pltpu.VMEM((count * TILE, NMO), jnp.bfloat16),
            pltpu.VMEM((NMO, count * TILE), jnp.bfloat16),
            pltpu.SMEM((count, SLOTS), jnp.int32),
            pltpu.SMEM((count * SLOTS + GROUP,), jnp.int32),
            pltpu.SemaphoreType.DMA((count * SLOTS, 2)),
            pltpu.SemaphoreType.DMA((2,)),
        ],
        compiler_params=pltpu.CompilerParams(vmem_limit_bytes=24 * MIB),
        cost_estimate=pl.CostEstimate(flops=2_000_000_000, bytes_accessed=12_000_000, transcendentals=0),
        name="tiles",
    )(*placed)


def outer(count, row, left, sigma, block):
    before, _, after = sides(count, row)
    slots = before if left else after
    if not slots:
        return None
    return contract(sigma, row, slots, block, row if left else row + slots[0] - BAND - count)


def prepare_kernel(count, piece, part, sigma, near, total):
    first = lax.rem(lax.axis_index("trow"), 2) == 0
    columns = slice(piece * COLUMNS, (piece + 1) * COLUMNS)

    def add(left):
        for row in range(count):
            value = part[row, :, columns]
            term = outer(count, row, left, sigma, near)
            total[row] = value if term is None else value + term

    @pl.when(first)
    def _():
        add(False)

    @pl.when(jnp.logical_not(first))
    def _():
        add(True)


def prepare(part, sigma, near, piece):
    count = part.shape[0]
    vmem = pl.BlockSpec(memory_space=pltpu.VMEM)
    return pl.pallas_call(
        functools.partial(prepare_kernel, count, piece),
        out_shape=pltpu.VMEM((count, PAIRS * TILE, COLUMNS), jnp.float32),
        in_specs=[vmem] * 3,
        out_specs=vmem,
        compiler_params=pltpu.CompilerParams(vmem_limit_bytes=16 * MIB),
        cost_estimate=pl.CostEstimate(flops=200_000_000, bytes_accessed=2_000_000, transcendentals=0),
        name="prepare",
    )(*[pltpu.with_memory_space_constraint(x, pltpu.VMEM) for x in (part, sigma, near)])


def project_kernel(count, split, *refs):
    part, sigma, *near, halo, transposed, out, half = refs
    first = lax.rem(lax.axis_index("trow"), 2) == 0

    def finish(far_left):
        for row in range(count):
            value = part[row, :, :COLUMNS]
            for left, block in [(not far_left, ref) for ref in near] + [(far_left, halo)]:
                term = outer(count, row, left, sigma, block)
                value = value if term is None else value + term
            for t in range(PAIRS):
                half[row * TILE : (row + 1) * TILE, t * COLUMNS : (t + 1) * COLUMNS] = value[
                    t * TILE : (t + 1) * TILE
                ].astype(jnp.bfloat16)

    @pl.when(first)
    def _():
        finish(True)

    @pl.when(jnp.logical_not(first))
    def _():
        finish(False)

    rows = slice(NMO // 2, NMO) if split else slice(0, NMO)
    out[...] = jnp.dot(transposed[rows, :], half[...], preferred_element_type=jnp.float32).astype(out.dtype)


def project(part, sigma, near, halo, transposed, split, piece):
    count = part.shape[0]
    if piece:
        operands = (prepare(part, sigma, near, piece), sigma, halo, transposed)
    else:
        operands = (part, sigma, near, halo, transposed)
    vmem = pl.BlockSpec(memory_space=pltpu.VMEM)
    if split:
        out_shape = pltpu.VMEM((NMO // 2, PAIRS * COLUMNS), jnp.bfloat16)
    else:
        out_shape = jax.ShapeDtypeStruct((NMO, PAIRS * COLUMNS), jnp.float32)
    return pl.pallas_call(
        functools.partial(project_kernel, count, split),
        out_shape=(out_shape, pltpu.VMEM((count * TILE, PAIRS * COLUMNS), jnp.bfloat16)),
        in_specs=[vmem] * len(operands),
        out_specs=(vmem, vmem),
        compiler_params=pltpu.CompilerParams(vmem_limit_bytes=16 * MIB),
        cost_estimate=pl.CostEstimate(flops=500_000_000, bytes_accessed=3_000_000, transcendentals=0),
        name="project",
    )(*[pltpu.with_memory_space_constraint(x, pltpu.VMEM) for x in operands])


def keep_kernel(half, transposed, out):
    out[...] = jnp.dot(transposed[: NMO // 2, :], half[...], preferred_element_type=jnp.float32)


def project_own(half, transposed):
    vmem = pl.BlockSpec(memory_space=pltpu.VMEM)
    return pl.pallas_call(
        keep_kernel,
        out_shape=pltpu.VMEM((NMO // 2, half.shape[1]), jnp.float32),
        in_specs=[vmem, vmem],
        out_specs=vmem,
        compiler_params=pltpu.CompilerParams(vmem_limit_bytes=16 * MIB),
        cost_estimate=pl.CostEstimate(flops=400_000_000, bytes_accessed=2_000_000, transcendentals=0),
        name="project_own",
    )(*[pltpu.with_memory_space_constraint(x, pltpu.VMEM) for x in (half, transposed)])


def freq_tables():
    point = np.arange(TAU, dtype=np.float32)
    freq = np.arange(NW, dtype=np.float32)
    pi = np.float32(np.pi)
    theta = pi * (np.float32(2.0) * point + np.float32(1.0)) / np.float32(2.0 * TAU)
    nodes = np.float32(0.5) * (np.float32(1.0) - np.cos(theta))
    weights = np.float32(np.pi / (2.0 * TAU)) * np.sin(theta)
    angle = pi * (np.float32(2.0) * freq[:, None] + np.float32(1.0)) * nodes[None, :]
    both = np.concatenate([weights[None, :] * np.cos(angle), weights[None, :] * np.sin(angle)], axis=0)
    folded = both[:, :PAIRS] + both[:, : PAIRS - 1 : -1]
    return np.repeat(folded.astype(np.float32).reshape(-1, 1), TILE, axis=1)


def frequency_kernel(terms, table, *refs):
    out, buffer, sems = refs[terms:]
    summed = refs[0][...]
    for ref in refs[1:terms]:
        summed = summed + ref[...].astype(jnp.float32)
    points = [
        jnp.concatenate(
            [summed[:, (piece * PAIRS + t) * COLUMNS : (piece * PAIRS + t + 1) * COLUMNS] for piece in range(CHUNKS)],
            axis=1,
        )
        for t in range(PAIRS)
    ]

    def number(at):
        return jnp.concatenate([table[pl.ds(at, 1), :]] * (NMO // TILE), axis=1)

    def transform(n):
        value = number(n * PAIRS) * points[0]
        for t in range(1, PAIRS):
            value = value + number(n * PAIRS + t) * points[t]
        buffer[n] = value

    copies = []
    for index, (begin, end) in enumerate(FREQ_BLOCKS):
        if end - begin <= FREQ_STEP:
            for n in range(begin, end):
                transform(n)
        else:
            pl.loop(begin, end, unroll=FREQ_STEP)(transform)
        copies.append(pltpu.make_async_copy(buffer.at[begin:end], out.at[begin:end], sems.at[index]))
        copies[-1].start()
    for copy in copies:
        copy.wait()


def frequency(*terms):
    rows = terms[0].shape[0]
    vmem = pl.BlockSpec(memory_space=pltpu.VMEM)
    out = pl.pallas_call(
        functools.partial(frequency_kernel, len(terms)),
        out_shape=jax.ShapeDtypeStruct((2 * NW, rows, NMO), jnp.float32),
        in_specs=[vmem] * (1 + len(terms)),
        out_specs=pl.BlockSpec(memory_space=pl.ANY),
        scratch_shapes=[
            pltpu.VMEM((2 * NW, rows, NMO), jnp.float32),
            pltpu.SemaphoreType.DMA((len(FREQ_BLOCKS),)),
        ],
        compiler_params=pltpu.CompilerParams(vmem_limit_bytes=24 * MIB),
        cost_estimate=pl.CostEstimate(flops=50_000_000, bytes_accessed=17_000_000, transcendentals=0),
        name="frequency",
    )(*[pltpu.with_memory_space_constraint(x, pltpu.VMEM) for x in (jnp.asarray(freq_tables()), *terms)])
    return out.reshape(2, NW, rows, NMO)


def local(devices, green, integrals, pattern, coefficients):
    rows = coefficients.shape[0]
    width = BAND * TILE
    core = lax.rem(lax.axis_index("trow"), 2)
    partner = [(i, i ^ 1) for i in range(devices)]
    pairs = [(i, i + 1) for i in range(1, devices - 1, 2)]
    pairs += [(b, a) for a, b in pairs]
    halos, nears = [], []
    for piece in range(CHUNKS):
        away = lax.dynamic_slice(coefficients, (core * (rows - width), piece * COLUMNS), (width, COLUMNS))
        halos.append(lax.ppermute(away, "trow", pairs))
        inner = lax.dynamic_slice(coefficients, ((1 - core) * (rows - width), piece * COLUMNS), (width, COLUMNS))
        nears.append(lax.ppermute(inner, "trow", partner))
    part, sigma, transposed = tiles(green, integrals, pattern, coefficients, devices == 16)
    if devices != 16:
        summed = jnp.concatenate(
            [project(part, sigma, nears[piece], halos[piece], transposed, False, piece)[0] for piece in range(CHUNKS)], axis=1
        )
        return frequency(lax.psum_scatter(summed, "trow", scatter_dimension=0, tiled=True))
    keeps, arrived = [], []
    for piece in range(CHUNKS):
        send, half = project(part, sigma, nears[piece], halos[piece], transposed, True, piece)
        arrived.append(lax.ppermute(send, "trow", partner))
        keeps.append(project_own(half, transposed))
    size = NMO // 16
    both = list(zip(keeps, arrived))
    sums = [
        jnp.concatenate(
            [keep[k * size : (k + 1) * size] + other[k * size : (k + 1) * size].astype(jnp.float32) for keep, other in both],
            axis=1,
        )
        for k in range(8)
    ]
    cast = [value.astype(jnp.bfloat16) for value in sums]
    flip = {k: [(i, i ^ (2 * k)) for i in range(devices)] for k in range(1, 8)}
    parts = []
    for keep, other in both:
        blocks = [
            keep[k * size : (k + 1) * size] + other[k * size : (k + 1) * size].astype(jnp.float32) for k in (1, 3, 5)
        ]
        parts.append(lax.ppermute(jnp.stack(blocks).astype(jnp.bfloat16), "trow", flip[1]))
    beside = jnp.concatenate(lax.optimization_barrier(parts), axis=2).astype(jnp.float32)
    straight = [lax.ppermute(cast[k], "trow", flip[k]) for k in (6, 7)]
    merged = [
        lax.ppermute((sums[k] + beside[at]).astype(jnp.bfloat16), "trow", flip[k]) for at, k in ((1, 2), (2, 4))
    ]
    terms = [sums[0] + beside[0], *straight, *merged]
    return frequency(*terms)


def solution(mesh):
    in_specs = (
        P(("flake", "trow"), None, None, None, None),
        P(("flake", "trow"), None, None, None),
        P(("flake", "trow"), None),
        P(("flake", "trow"), None),
    )
    out_specs = P(None, None, ("flake", "trow"), None)
    return jax.shard_map(
        functools.partial(local, mesh.shape["trow"]),
        mesh=mesh,
        in_specs=in_specs,
        out_specs=out_specs,
        check_vma=False,
    )
```

```python
import functools

import jax
import jax.numpy as jnp
import numpy as np
from jax import lax
from jax.experimental import pallas as pl
from jax.experimental.pallas import tpu as pltpu
from jax.sharding import PartitionSpec as P

TILE = 128
BAND = 4
TAU = 4
PAIRS = TAU // 2
NMO = 512
NW = 128
SLOTS = 9
FREQ_STEP = 4
FREQ_EDGES = [0, 2, 4, 8, 16, *range(32, 2 * NW + 1, 32)]
FREQ_BLOCKS = list(zip(FREQ_EDGES, FREQ_EDGES[1:]))
GROUP = 6
CHUNKS = 2
COLUMNS = NMO // CHUNKS
MIB = 1 << 20


def sides(count, row):
    return range(0, max(0, BAND - row)), range(max(0, BAND - row), min(SLOTS, count + BAND - row)), range(
        min(SLOTS, count + BAND - row), SLOTS
    )


def contract(sigma, row, slots, block, begin):
    lhs = jnp.concatenate([sigma[row, slot] for slot in slots], axis=1)
    rhs = block[begin * TILE : (begin + len(slots)) * TILE, :]
    return jnp.dot(lhs, rhs, preferred_element_type=jnp.float32)


def tiles_kernel(
    count,
    split,
    mask,
    green,
    integrals,
    coefficients,
    part,
    sigma,
    transposed,
    gbuf,
    ibuf,
    own,
    turned,
    pattern,
    order,
    sems,
    csem,
):
    def fetch(index):
        row, slot = index // SLOTS, index % SLOTS
        return (
            pltpu.make_async_copy(green.at[row, slot], gbuf.at[index], sems.at[index, 0]),
            pltpu.make_async_copy(integrals.at[row, slot], ibuf.at[index], sems.at[index, 1]),
        )

    def enlist(index, found):
        present = pattern[index // SLOTS, index % SLOTS] != 0

        @pl.when(present)
        def _():
            order[found] = index
            for copy in fetch(index):
                copy.start()

        return found + present.astype(jnp.int32)

    mask_copy = pltpu.make_async_copy(mask, pattern, csem.at[0])
    own_copy = pltpu.make_async_copy(coefficients, own, csem.at[1])
    mask_copy.start()
    own_copy.start()
    sigma[...] = jnp.zeros_like(sigma)
    mask_copy.wait()
    found = lax.fori_loop(0, count * SLOTS, enlist, jnp.int32(0))
    for extra in range(GROUP - 1):
        order[found + extra] = order[found - 1]
    own_copy.wait()
    for row in range(count):
        rows = slice(row * TILE, (row + 1) * TILE)
        (turned if split else transposed)[:, rows] = own[rows, :].T
    if split:
        place = lax.axis_index("trow")
        size = NMO // 16
        for k in range(16):
            owner = lax.bitwise_xor(place, 2 * (k % 8) + k // 8)
            transposed[k * size : (k + 1) * size, :] = turned[pl.ds(pl.multiple_of(owner * size, size), size), :]

    @pl.loop(0, pl.cdiv(found, GROUP))
    def _(group):
        indices = [order[group * GROUP + member] for member in range(GROUP)]
        for member, index in enumerate(indices):

            @pl.when(group * GROUP + member < found)
            def _():
                for copy in fetch(index):
                    copy.wait()

        for index in indices:
            paired = jnp.concatenate([gbuf[index, t] * gbuf[index, TAU - 1 - t] for t in range(PAIRS)], axis=0)
            product = jnp.dot(paired, ibuf[index], preferred_element_type=jnp.float32)
            sigma[index // SLOTS, index % SLOTS] = product.astype(jnp.bfloat16)

    for row in range(count):
        _, slots, _ = sides(count, row)
        part[row] = contract(sigma, row, slots, own, row + slots[0] - BAND)


def tiles(green, integrals, pattern, coefficients, split):
    count = green.shape[0]
    hbm = pl.BlockSpec(memory_space=pltpu.HBM)
    vmem = pl.BlockSpec(memory_space=pltpu.VMEM)
    placed = [pltpu.with_memory_space_constraint(x, pltpu.HBM) for x in (pattern, green, integrals, coefficients)]
    return pl.pallas_call(
        functools.partial(tiles_kernel, count, split),
        out_shape=(
            pltpu.VMEM((count, PAIRS * TILE, NMO), jnp.float32),
            pltpu.VMEM((count, SLOTS, PAIRS * TILE, TILE), jnp.bfloat16),
            pltpu.VMEM((NMO, count * TILE), jnp.bfloat16),
        ),
        in_specs=[hbm] * 4,
        out_specs=(vmem,) * 3,
        scratch_shapes=[
            pltpu.VMEM((count * SLOTS, TAU, TILE, TILE), jnp.bfloat16),
            pltpu.VMEM((count * SLOTS, TILE, TILE), jnp.bfloat16),
            pltpu.VMEM((count * TILE, NMO), jnp.bfloat16),
            pltpu.VMEM((NMO, count * TILE), jnp.bfloat16),
            pltpu.SMEM((count, SLOTS), jnp.int32),
            pltpu.SMEM((count * SLOTS + GROUP,), jnp.int32),
            pltpu.SemaphoreType.DMA((count * SLOTS, 2)),
            pltpu.SemaphoreType.DMA((2,)),
        ],
        compiler_params=pltpu.CompilerParams(vmem_limit_bytes=24 * MIB),
        cost_estimate=pl.CostEstimate(flops=2_000_000_000, bytes_accessed=12_000_000, transcendentals=0),
        name="tiles",
    )(*placed)


def outer(count, row, left, sigma, block):
    before, _, after = sides(count, row)
    slots = before if left else after
    if not slots:
        return None
    return contract(sigma, row, slots, block, row if left else row + slots[0] - BAND - count)


def prepare_kernel(count, piece, part, sigma, near, total):
    first = lax.rem(lax.axis_index("trow"), 2) == 0
    columns = slice(piece * COLUMNS, (piece + 1) * COLUMNS)

    def add(left):
        for row in range(count):
            value = part[row, :, columns]
            term = outer(count, row, left, sigma, near)
            total[row] = value if term is None else value + term

    @pl.when(first)
    def _():
        add(False)

    @pl.when(jnp.logical_not(first))
    def _():
        add(True)


def prepare(part, sigma, near, piece):
    count = part.shape[0]
    vmem = pl.BlockSpec(memory_space=pltpu.VMEM)
    return pl.pallas_call(
        functools.partial(prepare_kernel, count, piece),
        out_shape=pltpu.VMEM((count, PAIRS * TILE, COLUMNS), jnp.float32),
        in_specs=[vmem] * 3,
        out_specs=vmem,
        compiler_params=pltpu.CompilerParams(vmem_limit_bytes=16 * MIB),
        cost_estimate=pl.CostEstimate(flops=200_000_000, bytes_accessed=2_000_000, transcendentals=0),
        name="prepare",
    )(*[pltpu.with_memory_space_constraint(x, pltpu.VMEM) for x in (part, sigma, near)])


def project_kernel(count, split, *refs):
    part, sigma, *near, halo, transposed, out, half = refs
    first = lax.rem(lax.axis_index("trow"), 2) == 0

    def finish(far_left):
        for row in range(count):
            value = part[row, :, :COLUMNS]
            for left, block in [(not far_left, ref) for ref in near] + [(far_left, halo)]:
                term = outer(count, row, left, sigma, block)
                value = value if term is None else value + term
            for t in range(PAIRS):
                half[row * TILE : (row + 1) * TILE, t * COLUMNS : (t + 1) * COLUMNS] = value[
                    t * TILE : (t + 1) * TILE
                ].astype(jnp.bfloat16)

    @pl.when(first)
    def _():
        finish(True)

    @pl.when(jnp.logical_not(first))
    def _():
        finish(False)

    rows = slice(NMO // 2, NMO) if split else slice(0, NMO)
    out[...] = jnp.dot(transposed[rows, :], half[...], preferred_element_type=jnp.float32).astype(out.dtype)


def project(part, sigma, near, halo, transposed, split, piece):
    count = part.shape[0]
    if piece:
        operands = (prepare(part, sigma, near, piece), sigma, halo, transposed)
    else:
        operands = (part, sigma, near, halo, transposed)
    vmem = pl.BlockSpec(memory_space=pltpu.VMEM)
    if split:
        out_shape = pltpu.VMEM((NMO // 2, PAIRS * COLUMNS), jnp.bfloat16)
    else:
        out_shape = jax.ShapeDtypeStruct((NMO, PAIRS * COLUMNS), jnp.float32)
    return pl.pallas_call(
        functools.partial(project_kernel, count, split),
        out_shape=(out_shape, pltpu.VMEM((count * TILE, PAIRS * COLUMNS), jnp.bfloat16)),
        in_specs=[vmem] * len(operands),
        out_specs=(vmem, vmem),
        compiler_params=pltpu.CompilerParams(vmem_limit_bytes=16 * MIB),
        cost_estimate=pl.CostEstimate(flops=500_000_000, bytes_accessed=3_000_000, transcendentals=0),
        name="project",
    )(*[pltpu.with_memory_space_constraint(x, pltpu.VMEM) for x in operands])


def keep_kernel(half, transposed, out):
    out[...] = jnp.dot(transposed[: NMO // 2, :], half[...], preferred_element_type=jnp.float32)


def project_own(half, transposed):
    vmem = pl.BlockSpec(memory_space=pltpu.VMEM)
    return pl.pallas_call(
        keep_kernel,
        out_shape=pltpu.VMEM((NMO // 2, half.shape[1]), jnp.float32),
        in_specs=[vmem, vmem],
        out_specs=vmem,
        compiler_params=pltpu.CompilerParams(vmem_limit_bytes=16 * MIB),
        cost_estimate=pl.CostEstimate(flops=400_000_000, bytes_accessed=2_000_000, transcendentals=0),
        name="project_own",
    )(*[pltpu.with_memory_space_constraint(x, pltpu.VMEM) for x in (half, transposed)])


def freq_tables():
    point = np.arange(TAU, dtype=np.float32)
    freq = np.arange(NW, dtype=np.float32)
    pi = np.float32(np.pi)
    theta = pi * (np.float32(2.0) * point + np.float32(1.0)) / np.float32(2.0 * TAU)
    nodes = np.float32(0.5) * (np.float32(1.0) - np.cos(theta))
    weights = np.float32(np.pi / (2.0 * TAU)) * np.sin(theta)
    angle = pi * (np.float32(2.0) * freq[:, None] + np.float32(1.0)) * nodes[None, :]
    both = np.concatenate([weights[None, :] * np.cos(angle), weights[None, :] * np.sin(angle)], axis=0)
    folded = both[:, :PAIRS] + both[:, : PAIRS - 1 : -1]
    return np.repeat(folded.astype(np.float32).reshape(-1, 1), TILE, axis=1)


def frequency_kernel(terms, table, *refs):
    out, buffer, sems = refs[terms:]
    summed = refs[0][...]
    for ref in refs[1:terms]:
        summed = summed + ref[...].astype(jnp.float32)
    points = [
        jnp.concatenate(
            [summed[:, (piece * PAIRS + t) * COLUMNS : (piece * PAIRS + t + 1) * COLUMNS] for piece in range(CHUNKS)],
            axis=1,
        )
        for t in range(PAIRS)
    ]

    def number(at):
        return jnp.concatenate([table[pl.ds(at, 1), :]] * (NMO // TILE), axis=1)

    def transform(n):
        value = number(n * PAIRS) * points[0]
        for t in range(1, PAIRS):
            value = value + number(n * PAIRS + t) * points[t]
        buffer[n] = value

    copies = []
    for index, (begin, end) in enumerate(FREQ_BLOCKS):
        if end - begin <= FREQ_STEP:
            for n in range(begin, end):
                transform(n)
        else:
            pl.loop(begin, end, unroll=FREQ_STEP)(transform)
        copies.append(pltpu.make_async_copy(buffer.at[begin:end], out.at[begin:end], sems.at[index]))
        copies[-1].start()
    for copy in copies:
        copy.wait()


def frequency(*terms):
    rows = terms[0].shape[0]
    vmem = pl.BlockSpec(memory_space=pltpu.VMEM)
    out = pl.pallas_call(
        functools.partial(frequency_kernel, len(terms)),
        out_shape=jax.ShapeDtypeStruct((2 * NW, rows, NMO), jnp.float32),
        in_specs=[vmem] * (1 + len(terms)),
        out_specs=pl.BlockSpec(memory_space=pl.ANY),
        scratch_shapes=[
            pltpu.VMEM((2 * NW, rows, NMO), jnp.float32),
            pltpu.SemaphoreType.DMA((len(FREQ_BLOCKS),)),
        ],
        compiler_params=pltpu.CompilerParams(vmem_limit_bytes=24 * MIB),
        cost_estimate=pl.CostEstimate(flops=50_000_000, bytes_accessed=17_000_000, transcendentals=0),
        name="frequency",
    )(*[pltpu.with_memory_space_constraint(x, pltpu.VMEM) for x in (jnp.asarray(freq_tables()), *terms)])
    return out.reshape(2, NW, rows, NMO)


def local(devices, green, integrals, pattern, coefficients):
    rows = coefficients.shape[0]
    width = BAND * TILE
    core = lax.rem(lax.axis_index("trow"), 2)
    partner = [(i, i ^ 1) for i in range(devices)]
    pairs = [(i, i + 1) for i in range(1, devices - 1, 2)]
    pairs += [(b, a) for a, b in pairs]
    halos, nears = [], []
    for piece in range(CHUNKS):
        away = lax.dynamic_slice(coefficients, (core * (rows - width), piece * COLUMNS), (width, COLUMNS))
        halos.append(lax.ppermute(away, "trow", pairs))
        inner = lax.dynamic_slice(coefficients, ((1 - core) * (rows - width), piece * COLUMNS), (width, COLUMNS))
        nears.append(lax.ppermute(inner, "trow", partner))
    part, sigma, transposed = tiles(green, integrals, pattern, coefficients, devices == 16)
    if devices != 16:
        summed = jnp.concatenate(
            [project(part, sigma, nears[piece], halos[piece], transposed, False, piece)[0] for piece in range(CHUNKS)], axis=1
        )
        return frequency(lax.psum_scatter(summed, "trow", scatter_dimension=0, tiled=True))
    keeps, arrived = [], []
    for piece in range(CHUNKS):
        send, half = project(part, sigma, nears[piece], halos[piece], transposed, True, piece)
        arrived.append(lax.ppermute(send, "trow", partner))
        keeps.append(project_own(half, transposed))
    size = NMO // 16
    both = list(zip(keeps, arrived))
    sums = [
        jnp.concatenate(
            [keep[k * size : (k + 1) * size] + other[k * size : (k + 1) * size].astype(jnp.float32) for keep, other in both],
            axis=1,
        )
        for k in range(8)
    ]
    cast = [value.astype(jnp.bfloat16) for value in sums]
    flip = {k: [(i, i ^ (2 * k)) for i in range(devices)] for k in range(1, 8)}
    parts = []
    for keep, other in both:
        blocks = [
            keep[k * size : (k + 1) * size] + other[k * size : (k + 1) * size].astype(jnp.float32) for k in (1, 3, 5)
        ]
        parts.append(lax.ppermute(jnp.stack(blocks).astype(jnp.bfloat16), "trow", flip[1]))
    beside = jnp.concatenate(lax.optimization_barrier(parts), axis=2).astype(jnp.float32)
    straight = [lax.ppermute(cast[k], "trow", flip[k]) for k in (6, 7)]
    merged = [
        lax.ppermute((sums[k] + beside[at]).astype(jnp.bfloat16), "trow", flip[k]) for at, k in ((1, 2), (2, 4))
    ]
    terms = [sums[0] + beside[0], *straight, *merged]
    return frequency(*terms)


def solution(mesh):
    in_specs = (
        P(("flake", "trow"), None, None, None, None),
        P(("flake", "trow"), None, None, None),
        P(("flake", "trow"), None),
        P(("flake", "trow"), None),
    )
    out_specs = P(None, None, ("flake", "trow"), None)
    return jax.shard_map(
        functools.partial(local, mesh.shape["trow"]),
        mesh=mesh,
        in_specs=in_specs,
        out_specs=out_specs,
        check_vma=False,
    )
```

```python
import functools

import jax
import jax.numpy as jnp
import numpy as np
from jax import lax
from jax.experimental import pallas as pl
from jax.experimental.pallas import tpu as pltpu
from jax.sharding import PartitionSpec as P

TILE = 128
BAND = 4
TAU = 4
PAIRS = TAU // 2
NMO = 512
NW = 128
SLOTS = 9
FREQ_STEP = 4
FREQ_EDGES = [0, 2, 4, 8, 16, *range(32, 2 * NW + 1, 32)]
FREQ_BLOCKS = list(zip(FREQ_EDGES, FREQ_EDGES[1:]))
GROUP = 6
CHUNKS = 2
COLUMNS = NMO // CHUNKS
MIB = 1 << 20


def sides(count, row):
    return range(0, max(0, BAND - row)), range(max(0, BAND - row), min(SLOTS, count + BAND - row)), range(
        min(SLOTS, count + BAND - row), SLOTS
    )


def contract(sigma, row, slots, block, begin):
    lhs = jnp.concatenate([sigma[row, slot] for slot in slots], axis=1)
    rhs = block[begin * TILE : (begin + len(slots)) * TILE, :]
    return jnp.dot(lhs, rhs, preferred_element_type=jnp.float32)


def tiles_kernel(
    count,
    split,
    mask,
    green,
    integrals,
    coefficients,
    part,
    sigma,
    transposed,
    gbuf,
    ibuf,
    own,
    turned,
    pattern,
    order,
    sems,
    csem,
):
    def fetch(index):
        row, slot = index // SLOTS, index % SLOTS
        return (
            pltpu.make_async_copy(green.at[row, slot], gbuf.at[index], sems.at[index, 0]),
            pltpu.make_async_copy(integrals.at[row, slot], ibuf.at[index], sems.at[index, 1]),
        )

    def enlist(index, found):
        present = pattern[index // SLOTS, index % SLOTS] != 0

        @pl.when(present)
        def _():
            order[found] = index
            for copy in fetch(index):
                copy.start()

        return found + present.astype(jnp.int32)

    mask_copy = pltpu.make_async_copy(mask, pattern, csem.at[0])
    own_copy = pltpu.make_async_copy(coefficients, own, csem.at[1])
    mask_copy.start()
    own_copy.start()
    sigma[...] = jnp.zeros_like(sigma)
    mask_copy.wait()
    found = lax.fori_loop(0, count * SLOTS, enlist, jnp.int32(0))
    for extra in range(GROUP - 1):
        order[found + extra] = order[found - 1]
    own_copy.wait()
    for row in range(count):
        rows = slice(row * TILE, (row + 1) * TILE)
        (turned if split else transposed)[:, rows] = own[rows, :].T
    if split:
        place = lax.axis_index("trow")
        size = NMO // 16
        for k in range(16):
            owner = lax.bitwise_xor(place, 2 * (k % 8) + k // 8)
            transposed[k * size : (k + 1) * size, :] = turned[pl.ds(pl.multiple_of(owner * size, size), size), :]

    @pl.loop(0, pl.cdiv(found, GROUP))
    def _(group):
        indices = [order[group * GROUP + member] for member in range(GROUP)]
        for member, index in enumerate(indices):

            @pl.when(group * GROUP + member < found)
            def _():
                for copy in fetch(index):
                    copy.wait()

        for index in indices:
            paired = jnp.concatenate([gbuf[index, t] * gbuf[index, TAU - 1 - t] for t in range(PAIRS)], axis=0)
            product = jnp.dot(paired, ibuf[index], preferred_element_type=jnp.float32)
            sigma[index // SLOTS, index % SLOTS] = product.astype(jnp.bfloat16)

    for row in range(count):
        _, slots, _ = sides(count, row)
        part[row] = contract(sigma, row, slots, own, row + slots[0] - BAND)


def tiles(green, integrals, pattern, coefficients, split):
    count = green.shape[0]
    hbm = pl.BlockSpec(memory_space=pltpu.HBM)
    vmem = pl.BlockSpec(memory_space=pltpu.VMEM)
    placed = [pltpu.with_memory_space_constraint(x, pltpu.HBM) for x in (pattern, green, integrals, coefficients)]
    return pl.pallas_call(
        functools.partial(tiles_kernel, count, split),
        out_shape=(
            pltpu.VMEM((count, PAIRS * TILE, NMO), jnp.float32),
            pltpu.VMEM((count, SLOTS, PAIRS * TILE, TILE), jnp.bfloat16),
            pltpu.VMEM((NMO, count * TILE), jnp.bfloat16),
        ),
        in_specs=[hbm] * 4,
        out_specs=(vmem,) * 3,
        scratch_shapes=[
            pltpu.VMEM((count * SLOTS, TAU, TILE, TILE), jnp.bfloat16),
            pltpu.VMEM((count * SLOTS, TILE, TILE), jnp.bfloat16),
            pltpu.VMEM((count * TILE, NMO), jnp.bfloat16),
            pltpu.VMEM((NMO, count * TILE), jnp.bfloat16),
            pltpu.SMEM((count, SLOTS), jnp.int32),
            pltpu.SMEM((count * SLOTS + GROUP,), jnp.int32),
            pltpu.SemaphoreType.DMA((count * SLOTS, 2)),
            pltpu.SemaphoreType.DMA((2,)),
        ],
        compiler_params=pltpu.CompilerParams(vmem_limit_bytes=24 * MIB),
        cost_estimate=pl.CostEstimate(flops=2_000_000_000, bytes_accessed=12_000_000, transcendentals=0),
        name="tiles",
    )(*placed)


def outer(count, row, left, sigma, block):
    before, _, after = sides(count, row)
    slots = before if left else after
    if not slots:
        return None
    return contract(sigma, row, slots, block, row if left else row + slots[0] - BAND - count)


def prepare_kernel(count, piece, part, sigma, near, total):
    first = lax.rem(lax.axis_index("trow"), 2) == 0
    columns = slice(piece * COLUMNS, (piece + 1) * COLUMNS)

    def add(left):
        for row in range(count):
            value = part[row, :, columns]
            term = outer(count, row, left, sigma, near.at[:, columns])
            total[row] = value if term is None else value + term

    @pl.when(first)
    def _():
        add(False)

    @pl.when(jnp.logical_not(first))
    def _():
        add(True)


def prepare(part, sigma, near, piece):
    count = part.shape[0]
    vmem = pl.BlockSpec(memory_space=pltpu.VMEM)
    return pl.pallas_call(
        functools.partial(prepare_kernel, count, piece),
        out_shape=pltpu.VMEM((count, PAIRS * TILE, COLUMNS), jnp.float32),
        in_specs=[vmem] * 3,
        out_specs=vmem,
        compiler_params=pltpu.CompilerParams(vmem_limit_bytes=16 * MIB),
        cost_estimate=pl.CostEstimate(flops=200_000_000, bytes_accessed=2_000_000, transcendentals=0),
        name="prepare",
    )(*[pltpu.with_memory_space_constraint(x, pltpu.VMEM) for x in (part, sigma, near)])


def project_kernel(count, split, *refs):
    part, sigma, *near, halo, transposed, out, half = refs
    first = lax.rem(lax.axis_index("trow"), 2) == 0

    def finish(far_left):
        for row in range(count):
            value = part[row, :, :COLUMNS]
            for left, block in [(not far_left, ref.at[:, :COLUMNS]) for ref in near] + [(far_left, halo)]:
                term = outer(count, row, left, sigma, block)
                value = value if term is None else value + term
            for t in range(PAIRS):
                half[row * TILE : (row + 1) * TILE, t * COLUMNS : (t + 1) * COLUMNS] = value[
                    t * TILE : (t + 1) * TILE
                ].astype(jnp.bfloat16)

    @pl.when(first)
    def _():
        finish(True)

    @pl.when(jnp.logical_not(first))
    def _():
        finish(False)

    rows = slice(NMO // 2, NMO) if split else slice(0, NMO)
    out[...] = jnp.dot(transposed[rows, :], half[...], preferred_element_type=jnp.float32).astype(out.dtype)


def project(part, sigma, near, halo, transposed, split, piece):
    count = part.shape[0]
    if piece:
        operands = (prepare(part, sigma, near, piece), sigma, halo, transposed)
    else:
        operands = (part, sigma, near, halo, transposed)
    vmem = pl.BlockSpec(memory_space=pltpu.VMEM)
    if split:
        out_shape = pltpu.VMEM((NMO // 2, PAIRS * COLUMNS), jnp.bfloat16)
    else:
        out_shape = jax.ShapeDtypeStruct((NMO, PAIRS * COLUMNS), jnp.float32)
    return pl.pallas_call(
        functools.partial(project_kernel, count, split),
        out_shape=(out_shape, pltpu.VMEM((count * TILE, PAIRS * COLUMNS), jnp.bfloat16)),
        in_specs=[vmem] * len(operands),
        out_specs=(vmem, vmem),
        compiler_params=pltpu.CompilerParams(vmem_limit_bytes=16 * MIB),
        cost_estimate=pl.CostEstimate(flops=500_000_000, bytes_accessed=3_000_000, transcendentals=0),
        name="project",
    )(*[pltpu.with_memory_space_constraint(x, pltpu.VMEM) for x in operands])


def keep_kernel(half, transposed, out):
    out[...] = jnp.dot(transposed[: NMO // 2, :], half[...], preferred_element_type=jnp.float32)


def project_own(half, transposed):
    vmem = pl.BlockSpec(memory_space=pltpu.VMEM)
    return pl.pallas_call(
        keep_kernel,
        out_shape=pltpu.VMEM((NMO // 2, half.shape[1]), jnp.float32),
        in_specs=[vmem, vmem],
        out_specs=vmem,
        compiler_params=pltpu.CompilerParams(vmem_limit_bytes=16 * MIB),
        cost_estimate=pl.CostEstimate(flops=400_000_000, bytes_accessed=2_000_000, transcendentals=0),
        name="project_own",
    )(*[pltpu.with_memory_space_constraint(x, pltpu.VMEM) for x in (half, transposed)])


def freq_tables():
    point = np.arange(TAU, dtype=np.float32)
    freq = np.arange(NW, dtype=np.float32)
    pi = np.float32(np.pi)
    theta = pi * (np.float32(2.0) * point + np.float32(1.0)) / np.float32(2.0 * TAU)
    nodes = np.float32(0.5) * (np.float32(1.0) - np.cos(theta))
    weights = np.float32(np.pi / (2.0 * TAU)) * np.sin(theta)
    angle = pi * (np.float32(2.0) * freq[:, None] + np.float32(1.0)) * nodes[None, :]
    both = np.concatenate([weights[None, :] * np.cos(angle), weights[None, :] * np.sin(angle)], axis=0)
    folded = both[:, :PAIRS] + both[:, : PAIRS - 1 : -1]
    return np.repeat(folded.astype(np.float32).reshape(-1, 1), TILE, axis=1)


def frequency_kernel(terms, table, *refs):
    out, buffer, sems = refs[terms:]
    summed = refs[0][...]
    for ref in refs[1:terms]:
        summed = summed + ref[...].astype(jnp.float32)
    points = [
        jnp.concatenate(
            [summed[:, (piece * PAIRS + t) * COLUMNS : (piece * PAIRS + t + 1) * COLUMNS] for piece in range(CHUNKS)],
            axis=1,
        )
        for t in range(PAIRS)
    ]

    def number(at):
        return jnp.concatenate([table[pl.ds(at, 1), :]] * (NMO // TILE), axis=1)

    def transform(n):
        value = number(n * PAIRS) * points[0]
        for t in range(1, PAIRS):
            value = value + number(n * PAIRS + t) * points[t]
        buffer[n] = value

    copies = []
    for index, (begin, end) in enumerate(FREQ_BLOCKS):
        if end - begin <= FREQ_STEP:
            for n in range(begin, end):
                transform(n)
        else:
            pl.loop(begin, end, unroll=FREQ_STEP)(transform)
        copies.append(pltpu.make_async_copy(buffer.at[begin:end], out.at[begin:end], sems.at[index]))
        copies[-1].start()
    for copy in copies:
        copy.wait()


def frequency(*terms):
    rows = terms[0].shape[0]
    vmem = pl.BlockSpec(memory_space=pltpu.VMEM)
    out = pl.pallas_call(
        functools.partial(frequency_kernel, len(terms)),
        out_shape=jax.ShapeDtypeStruct((2 * NW, rows, NMO), jnp.float32),
        in_specs=[vmem] * (1 + len(terms)),
        out_specs=pl.BlockSpec(memory_space=pl.ANY),
        scratch_shapes=[
            pltpu.VMEM((2 * NW, rows, NMO), jnp.float32),
            pltpu.SemaphoreType.DMA((len(FREQ_BLOCKS),)),
        ],
        compiler_params=pltpu.CompilerParams(vmem_limit_bytes=24 * MIB),
        cost_estimate=pl.CostEstimate(flops=50_000_000, bytes_accessed=17_000_000, transcendentals=0),
        name="frequency",
    )(*[pltpu.with_memory_space_constraint(x, pltpu.VMEM) for x in (jnp.asarray(freq_tables()), *terms)])
    return out.reshape(2, NW, rows, NMO)


def local(devices, green, integrals, pattern, coefficients):
    rows = coefficients.shape[0]
    width = BAND * TILE
    core = lax.rem(lax.axis_index("trow"), 2)
    partner = [(i, i ^ 1) for i in range(devices)]
    pairs = [(i, i + 1) for i in range(1, devices - 1, 2)]
    pairs += [(b, a) for a, b in pairs]
    halos = []
    for piece in range(CHUNKS):
        away = lax.dynamic_slice(coefficients, (core * (rows - width), piece * COLUMNS), (width, COLUMNS))
        halos.append(lax.ppermute(away, "trow", pairs))
    inner = lax.dynamic_slice_in_dim(coefficients, (1 - core) * (rows - width), width, axis=0)
    near = lax.ppermute(inner, "trow", partner)
    nears = [near] * CHUNKS
    part, sigma, transposed = tiles(green, integrals, pattern, coefficients, devices == 16)
    if devices != 16:
        summed = jnp.concatenate(
            [project(part, sigma, nears[piece], halos[piece], transposed, False, piece)[0] for piece in range(CHUNKS)], axis=1
        )
        return frequency(lax.psum_scatter(summed, "trow", scatter_dimension=0, tiled=True))
    keeps, arrived = [], []
    for piece in range(CHUNKS):
        send, half = project(part, sigma, nears[piece], halos[piece], transposed, True, piece)
        arrived.append(lax.ppermute(send, "trow", partner))
        keeps.append(project_own(half, transposed))
    size = NMO // 16
    both = list(zip(keeps, arrived))
    sums = [
        jnp.concatenate(
            [keep[k * size : (k + 1) * size] + other[k * size : (k + 1) * size].astype(jnp.float32) for keep, other in both],
            axis=1,
        )
        for k in range(8)
    ]
    cast = [value.astype(jnp.bfloat16) for value in sums]
    flip = {k: [(i, i ^ (2 * k)) for i in range(devices)] for k in range(1, 8)}
    parts = []
    for keep, other in both:
        blocks = [
            keep[k * size : (k + 1) * size] + other[k * size : (k + 1) * size].astype(jnp.float32) for k in (1, 3, 5)
        ]
        parts.append(lax.ppermute(jnp.stack(blocks).astype(jnp.bfloat16), "trow", flip[1]))
    beside = jnp.concatenate(lax.optimization_barrier(parts), axis=2).astype(jnp.float32)
    straight = [lax.ppermute(cast[k], "trow", flip[k]) for k in (6, 7)]
    merged = [
        lax.ppermute((sums[k] + beside[at]).astype(jnp.bfloat16), "trow", flip[k]) for at, k in ((1, 2), (2, 4))
    ]
    terms = [sums[0] + beside[0], *straight, *merged]
    return frequency(*terms)


def solution(mesh):
    in_specs = (
        P(("flake", "trow"), None, None, None, None),
        P(("flake", "trow"), None, None, None),
        P(("flake", "trow"), None),
        P(("flake", "trow"), None),
    )
    out_specs = P(None, None, ("flake", "trow"), None)
    return jax.shard_map(
        functools.partial(local, mesh.shape["trow"]),
        mesh=mesh,
        in_specs=in_specs,
        out_specs=out_specs,
        check_vma=False,
    )
```

```python
import functools

import jax
import jax.numpy as jnp
import numpy as np
from jax import lax
from jax.experimental import pallas as pl
from jax.experimental.pallas import tpu as pltpu
from jax.sharding import PartitionSpec as P

TILE = 128
BAND = 4
TAU = 4
PAIRS = TAU // 2
NMO = 512
NW = 128
SLOTS = 9
FREQ_STEP = 4
FREQ_EDGES = [0, 2, 4, 8, 16, *range(32, 2 * NW + 1, 32)]
FREQ_BLOCKS = list(zip(FREQ_EDGES, FREQ_EDGES[1:]))
GROUP = 9
CHUNKS = 2
COLUMNS = NMO // CHUNKS
MIB = 1 << 20


def sides(count, row):
    return range(0, max(0, BAND - row)), range(max(0, BAND - row), min(SLOTS, count + BAND - row)), range(
        min(SLOTS, count + BAND - row), SLOTS
    )


def contract(sigma, row, slots, block, begin):
    lhs = jnp.concatenate([sigma[row, slot] for slot in slots], axis=1)
    rhs = block[begin * TILE : (begin + len(slots)) * TILE, :]
    return jnp.dot(lhs, rhs, preferred_element_type=jnp.float32)


def tiles_kernel(
    count,
    split,
    mask,
    green,
    integrals,
    coefficients,
    part,
    sigma,
    transposed,
    gbuf,
    ibuf,
    own,
    turned,
    pattern,
    order,
    sems,
    csem,
):
    def fetch(index):
        row, slot = index // SLOTS, index % SLOTS
        return (
            pltpu.make_async_copy(green.at[row, slot], gbuf.at[index], sems.at[index, 0]),
            pltpu.make_async_copy(integrals.at[row, slot], ibuf.at[index], sems.at[index, 1]),
        )

    def enlist(index, found):
        present = pattern[index // SLOTS, index % SLOTS] != 0

        @pl.when(present)
        def _():
            order[found] = index
            for copy in fetch(index):
                copy.start()

        return found + present.astype(jnp.int32)

    mask_copy = pltpu.make_async_copy(mask, pattern, csem.at[0])
    own_copy = pltpu.make_async_copy(coefficients, own, csem.at[1])
    mask_copy.start()
    own_copy.start()
    sigma[...] = jnp.zeros_like(sigma)
    mask_copy.wait()
    found = lax.fori_loop(0, count * SLOTS, enlist, jnp.int32(0))
    for extra in range(GROUP - 1):
        order[found + extra] = order[found - 1]
    own_copy.wait()
    for row in range(count):
        rows = slice(row * TILE, (row + 1) * TILE)
        (turned if split else transposed)[:, rows] = own[rows, :].T
    if split:
        place = lax.axis_index("trow")
        size = NMO // 16
        for k in range(16):
            owner = lax.bitwise_xor(place, 2 * (k % 8) + k // 8)
            transposed[k * size : (k + 1) * size, :] = turned[pl.ds(pl.multiple_of(owner * size, size), size), :]

    @pl.loop(0, pl.cdiv(found, GROUP))
    def _(group):
        indices = [order[group * GROUP + member] for member in range(GROUP)]
        for member, index in enumerate(indices):

            @pl.when(group * GROUP + member < found)
            def _():
                for copy in fetch(index):
                    copy.wait()

        for index in indices:
            paired = jnp.concatenate([gbuf[index, t] * gbuf[index, TAU - 1 - t] for t in range(PAIRS)], axis=0)
            product = jnp.dot(paired, ibuf[index], preferred_element_type=jnp.float32)
            sigma[index // SLOTS, index % SLOTS] = product.astype(jnp.bfloat16)

    for row in range(count):
        _, slots, _ = sides(count, row)
        part[row] = contract(sigma, row, slots, own, row + slots[0] - BAND)


def tiles(green, integrals, pattern, coefficients, split):
    count = green.shape[0]
    hbm = pl.BlockSpec(memory_space=pltpu.HBM)
    vmem = pl.BlockSpec(memory_space=pltpu.VMEM)
    placed = [pltpu.with_memory_space_constraint(x, pltpu.HBM) for x in (pattern, green, integrals, coefficients)]
    return pl.pallas_call(
        functools.partial(tiles_kernel, count, split),
        out_shape=(
            pltpu.VMEM((count, PAIRS * TILE, NMO), jnp.float32),
            pltpu.VMEM((count, SLOTS, PAIRS * TILE, TILE), jnp.bfloat16),
            pltpu.VMEM((NMO, count * TILE), jnp.bfloat16),
        ),
        in_specs=[hbm] * 4,
        out_specs=(vmem,) * 3,
        scratch_shapes=[
            pltpu.VMEM((count * SLOTS, TAU, TILE, TILE), jnp.bfloat16),
            pltpu.VMEM((count * SLOTS, TILE, TILE), jnp.bfloat16),
            pltpu.VMEM((count * TILE, NMO), jnp.bfloat16),
            pltpu.VMEM((NMO, count * TILE), jnp.bfloat16),
            pltpu.SMEM((count, SLOTS), jnp.int32),
            pltpu.SMEM((count * SLOTS + GROUP,), jnp.int32),
            pltpu.SemaphoreType.DMA((count * SLOTS, 2)),
            pltpu.SemaphoreType.DMA((2,)),
        ],
        compiler_params=pltpu.CompilerParams(vmem_limit_bytes=24 * MIB),
        cost_estimate=pl.CostEstimate(flops=2_000_000_000, bytes_accessed=12_000_000, transcendentals=0),
        name="tiles",
    )(*placed)


def outer(count, row, left, sigma, block):
    before, _, after = sides(count, row)
    slots = before if left else after
    if not slots:
        return None
    return contract(sigma, row, slots, block, row if left else row + slots[0] - BAND - count)


def prepare_kernel(count, piece, part, sigma, near, total):
    first = lax.rem(lax.axis_index("trow"), 2) == 0
    columns = slice(piece * COLUMNS, (piece + 1) * COLUMNS)

    def add(left):
        for row in range(count):
            value = part[row, :, columns]
            term = outer(count, row, left, sigma, near)
            total[row] = value if term is None else value + term

    @pl.when(first)
    def _():
        add(False)

    @pl.when(jnp.logical_not(first))
    def _():
        add(True)


def prepare(part, sigma, near, piece):
    count = part.shape[0]
    vmem = pl.BlockSpec(memory_space=pltpu.VMEM)
    return pl.pallas_call(
        functools.partial(prepare_kernel, count, piece),
        out_shape=pltpu.VMEM((count, PAIRS * TILE, COLUMNS), jnp.float32),
        in_specs=[vmem] * 3,
        out_specs=vmem,
        compiler_params=pltpu.CompilerParams(vmem_limit_bytes=16 * MIB),
        cost_estimate=pl.CostEstimate(flops=200_000_000, bytes_accessed=2_000_000, transcendentals=0),
        name="prepare",
    )(*[pltpu.with_memory_space_constraint(x, pltpu.VMEM) for x in (part, sigma, near)])


def project_kernel(count, split, *refs):
    part, sigma, *near, halo, transposed, out, half = refs
    first = lax.rem(lax.axis_index("trow"), 2) == 0

    def finish(far_left):
        for row in range(count):
            value = part[row, :, :COLUMNS]
            for left, block in [(not far_left, ref) for ref in near] + [(far_left, halo)]:
                term = outer(count, row, left, sigma, block)
                value = value if term is None else value + term
            for t in range(PAIRS):
                half[row * TILE : (row + 1) * TILE, t * COLUMNS : (t + 1) * COLUMNS] = value[
                    t * TILE : (t + 1) * TILE
                ].astype(jnp.bfloat16)

    @pl.when(first)
    def _():
        finish(True)

    @pl.when(jnp.logical_not(first))
    def _():
        finish(False)

    rows = slice(NMO // 2, NMO) if split else slice(0, NMO)
    out[...] = jnp.dot(transposed[rows, :], half[...], preferred_element_type=jnp.float32).astype(out.dtype)


def project(part, sigma, near, halo, transposed, split, piece):
    count = part.shape[0]
    if piece:
        operands = (prepare(part, sigma, near, piece), sigma, halo, transposed)
    else:
        operands = (part, sigma, near, halo, transposed)
    vmem = pl.BlockSpec(memory_space=pltpu.VMEM)
    if split:
        out_shape = pltpu.VMEM((NMO // 2, PAIRS * COLUMNS), jnp.bfloat16)
    else:
        out_shape = jax.ShapeDtypeStruct((NMO, PAIRS * COLUMNS), jnp.float32)
    return pl.pallas_call(
        functools.partial(project_kernel, count, split),
        out_shape=(out_shape, pltpu.VMEM((count * TILE, PAIRS * COLUMNS), jnp.bfloat16)),
        in_specs=[vmem] * len(operands),
        out_specs=(vmem, vmem),
        compiler_params=pltpu.CompilerParams(vmem_limit_bytes=16 * MIB),
        cost_estimate=pl.CostEstimate(flops=500_000_000, bytes_accessed=3_000_000, transcendentals=0),
        name="project",
    )(*[pltpu.with_memory_space_constraint(x, pltpu.VMEM) for x in operands])


def keep_kernel(half, transposed, out):
    out[...] = jnp.dot(transposed[: NMO // 2, :], half[...], preferred_element_type=jnp.float32)


def project_own(half, transposed):
    vmem = pl.BlockSpec(memory_space=pltpu.VMEM)
    return pl.pallas_call(
        keep_kernel,
        out_shape=pltpu.VMEM((NMO // 2, half.shape[1]), jnp.float32),
        in_specs=[vmem, vmem],
        out_specs=vmem,
        compiler_params=pltpu.CompilerParams(vmem_limit_bytes=16 * MIB),
        cost_estimate=pl.CostEstimate(flops=400_000_000, bytes_accessed=2_000_000, transcendentals=0),
        name="project_own",
    )(*[pltpu.with_memory_space_constraint(x, pltpu.VMEM) for x in (half, transposed)])


def freq_tables():
    point = np.arange(TAU, dtype=np.float32)
    freq = np.arange(NW, dtype=np.float32)
    pi = np.float32(np.pi)
    theta = pi * (np.float32(2.0) * point + np.float32(1.0)) / np.float32(2.0 * TAU)
    nodes = np.float32(0.5) * (np.float32(1.0) - np.cos(theta))
    weights = np.float32(np.pi / (2.0 * TAU)) * np.sin(theta)
    angle = pi * (np.float32(2.0) * freq[:, None] + np.float32(1.0)) * nodes[None, :]
    both = np.concatenate([weights[None, :] * np.cos(angle), weights[None, :] * np.sin(angle)], axis=0)
    folded = both[:, :PAIRS] + both[:, : PAIRS - 1 : -1]
    return np.repeat(folded.astype(np.float32).reshape(-1, 1), TILE, axis=1)


def frequency_kernel(terms, table, *refs):
    out, buffer, sems = refs[terms:]
    summed = refs[0][...]
    for ref in refs[1:terms]:
        summed = summed + ref[...].astype(jnp.float32)
    points = [
        jnp.concatenate(
            [summed[:, (piece * PAIRS + t) * COLUMNS : (piece * PAIRS + t + 1) * COLUMNS] for piece in range(CHUNKS)],
            axis=1,
        )
        for t in range(PAIRS)
    ]

    def number(at):
        return jnp.concatenate([table[pl.ds(at, 1), :]] * (NMO // TILE), axis=1)

    def transform(n):
        value = number(n * PAIRS) * points[0]
        for t in range(1, PAIRS):
            value = value + number(n * PAIRS + t) * points[t]
        buffer[n] = value

    copies = []
    for index, (begin, end) in enumerate(FREQ_BLOCKS):
        if end - begin <= FREQ_STEP:
            for n in range(begin, end):
                transform(n)
        else:
            pl.loop(begin, end, unroll=FREQ_STEP)(transform)
        copies.append(pltpu.make_async_copy(buffer.at[begin:end], out.at[begin:end], sems.at[index]))
        copies[-1].start()
    for copy in copies:
        copy.wait()


def frequency(*terms):
    rows = terms[0].shape[0]
    vmem = pl.BlockSpec(memory_space=pltpu.VMEM)
    out = pl.pallas_call(
        functools.partial(frequency_kernel, len(terms)),
        out_shape=jax.ShapeDtypeStruct((2 * NW, rows, NMO), jnp.float32),
        in_specs=[vmem] * (1 + len(terms)),
        out_specs=pl.BlockSpec(memory_space=pl.ANY),
        scratch_shapes=[
            pltpu.VMEM((2 * NW, rows, NMO), jnp.float32),
            pltpu.SemaphoreType.DMA((len(FREQ_BLOCKS),)),
        ],
        compiler_params=pltpu.CompilerParams(vmem_limit_bytes=24 * MIB),
        cost_estimate=pl.CostEstimate(flops=50_000_000, bytes_accessed=17_000_000, transcendentals=0),
        name="frequency",
    )(*[pltpu.with_memory_space_constraint(x, pltpu.VMEM) for x in (jnp.asarray(freq_tables()), *terms)])
    return out.reshape(2, NW, rows, NMO)


def local(devices, green, integrals, pattern, coefficients):
    rows = coefficients.shape[0]
    width = BAND * TILE
    core = lax.rem(lax.axis_index("trow"), 2)
    partner = [(i, i ^ 1) for i in range(devices)]
    pairs = [(i, i + 1) for i in range(1, devices - 1, 2)]
    pairs += [(b, a) for a, b in pairs]
    halos, nears = [], []
    for piece in range(CHUNKS):
        away = lax.dynamic_slice(coefficients, (core * (rows - width), piece * COLUMNS), (width, COLUMNS))
        halos.append(lax.ppermute(away, "trow", pairs))
        inner = lax.dynamic_slice(coefficients, ((1 - core) * (rows - width), piece * COLUMNS), (width, COLUMNS))
        nears.append(lax.ppermute(inner, "trow", partner))
    part, sigma, transposed = tiles(green, integrals, pattern, coefficients, devices == 16)
    if devices != 16:
        summed = jnp.concatenate(
            [project(part, sigma, nears[piece], halos[piece], transposed, False, piece)[0] for piece in range(CHUNKS)], axis=1
        )
        return frequency(lax.psum_scatter(summed, "trow", scatter_dimension=0, tiled=True))
    keeps, arrived = [], []
    for piece in range(CHUNKS):
        send, half = project(part, sigma, nears[piece], halos[piece], transposed, True, piece)
        arrived.append(lax.ppermute(send, "trow", partner))
        keeps.append(project_own(half, transposed))
    size = NMO // 16
    both = list(zip(keeps, arrived))
    sums = [
        jnp.concatenate(
            [keep[k * size : (k + 1) * size] + other[k * size : (k + 1) * size].astype(jnp.float32) for keep, other in both],
            axis=1,
        )
        for k in range(8)
    ]
    cast = [value.astype(jnp.bfloat16) for value in sums]
    flip = {k: [(i, i ^ (2 * k)) for i in range(devices)] for k in range(1, 8)}
    parts = []
    for keep, other in both:
        blocks = [
            keep[k * size : (k + 1) * size] + other[k * size : (k + 1) * size].astype(jnp.float32) for k in (1, 3, 5)
        ]
        parts.append(lax.ppermute(jnp.stack(blocks).astype(jnp.bfloat16), "trow", flip[1]))
    beside = jnp.concatenate(lax.optimization_barrier(parts), axis=2).astype(jnp.float32)
    straight = [lax.ppermute(cast[k], "trow", flip[k]) for k in (6, 7)]
    merged = [
        lax.ppermute((sums[k] + beside[at]).astype(jnp.bfloat16), "trow", flip[k]) for at, k in ((1, 2), (2, 4))
    ]
    terms = [sums[0] + beside[0], *straight, *merged]
    return frequency(*terms)


def solution(mesh):
    in_specs = (
        P(("flake", "trow"), None, None, None, None),
        P(("flake", "trow"), None, None, None),
        P(("flake", "trow"), None),
        P(("flake", "trow"), None),
    )
    out_specs = P(None, None, ("flake", "trow"), None)
    return jax.shard_map(
        functools.partial(local, mesh.shape["trow"]),
        mesh=mesh,
        in_specs=in_specs,
        out_specs=out_specs,
        check_vma=False,
    )
```
